256 devices in a mesh: tok: 64 (over z, y, core), hid: 4 (over x).
Axes of the slice: x: 4, y: 4, z: 8, core: 2. Of those that a mesh axis runs over, the one named last changes fastest.
Arguments:
- tokens: bfloat16 [32768, 1024], P('tok', 'hid'), may hold values from -6 to 6
- width_index: int32 [32768], P('tok'), may hold values from 0 to 3, as said below
- up_weight: bfloat16 [1024, 4096], P('tok', 'hid'), may hold values from -0.1875 to 0.1875
- down_weight: bfloat16 [4096, 1024], P('hid', 'tok'), may hold values from -0.1875 to 0.1875
- cotangent: bfloat16 [32768, 1024], P('tok', 'hid'), may hold values from -6 to 6
Outputs:
- mixed: bfloat16 [32768, 1024], P('tok', 'hid')
- grad_tokens: bfloat16 [32768, 1024], P('tok', 'hid')
- grad_up: float32 [1024, 4096], P('tok', 'hid')
- grad_down: float32 [4096, 1024], P('hid', 'tok')
The draws below stay inside these ranges and needn't reach their ends.
Inputs may be any that keep to these rules, and one draw needn't show every extreme that they name: `width_index`: on each index of tok (its 512 tokens), at most 256 tokens have width index 1 or more, at most 128 have 2 or more and at most 64 have 3; in every draw some index of tok holds exactly 256, 128 and 64 such tokens.
All inputs are finite; a program needn't handle non-finite values.
Results may differ from the reference program's by a relative error of at most 0.0049.
Values may be sent and summed in bfloat16 or wider, within the bound.
A program may use at most 128 MiB of HBM per device.

```python
import math
import jax
import jax.numpy as jnp
from jax import lax

D = 1024
FF = 4096
TOK_DEV = 512
TOKENS = 32768


def draw_width_index(key, part):
    key = jax.random.fold_in(key, 11)
    device_count = TOKENS // TOK_DEV
    key_three, key_two, key_one, key_top, key_perm = jax.random.split(key, 5)
    most_three = TOK_DEV // 8
    most_two = TOK_DEV // 4
    most_one = TOK_DEV // 2
    count_three = jax.random.randint(key_three, (device_count,), most_three // 2, most_three + 1)
    count_two = jax.random.randint(key_two, (device_count,), most_two // 2, most_two + 1)
    count_one = jax.random.randint(key_one, (device_count,), most_one // 2, most_one + 1)
    chosen = jax.random.randint(key_top, (), 0, device_count)
    at_top = jnp.arange(device_count) == chosen
    count_three = jnp.where(at_top, most_three, count_three)
    count_two = jnp.where(at_top, most_two, count_two)
    count_one = jnp.where(at_top, most_one, count_one)
    perm_keys = jax.random.split(key_perm, device_count)
    ranks = jax.vmap(lambda single: jax.random.permutation(single, TOK_DEV))(perm_keys)
    levels = (ranks < count_three[:, None]).astype(jnp.int32)
    levels = levels + (ranks < count_two[:, None]).astype(jnp.int32)
    levels = levels + (ranks < count_one[:, None]).astype(jnp.int32)
    return levels.reshape(TOKENS).astype(jnp.int32)


def shard_levels(key, shape, pieces, smallest, high):
    gain = 1.0
    for axis_at, shards_of in pieces:
        draws = jax.random.uniform(jax.random.fold_in(jax.random.fold_in(key, 6), axis_at), (shards_of,), jnp.float32, smallest / len(pieces), high / len(pieces))
        gain = gain * jnp.repeat(jnp.exp(draws), shape[axis_at] // shards_of).reshape((-1,) + (1,) * (len(shape) - 1 - axis_at))
    return gain


def gaussian(stream_key, dims, deviation, bound, pieces=(), kind=jnp.bfloat16):
    values = jax.random.normal(stream_key, dims, jnp.float32) * deviation
    if len(pieces) > 0:
        values = shard_levels(stream_key, dims, pieces, -0.22, 0.18) * values
    return jnp.clip(values, min=-bound, max=bound).astype(kind)


def setup_inputs(seed: int = 0) -> dict:
    splits = jax.random.split(jax.random.key(seed), 6)
    tokens = gaussian(splits[0], (TOKENS, D), 1.0, 6.0, ((0, 64), (1, 4)))
    width_index = draw_width_index(jax.random.fold_in(splits[5], 71), 0)
    up_weight = gaussian(splits[2], (D, FF), D ** -0.5, 0.1875, ((0, 64), (1, 4)))
    down_weight = gaussian(splits[3], (FF, D), (FF // 4) ** -0.5, 0.1875, ((0, 4), (1, 64)))
    cotangent = gaussian(splits[4], (TOKENS, D), 1.0, 6.0, ((0, 64), (1, 4)))
    return dict(tokens=tokens, width_index=width_index, up_weight=up_weight, down_weight=down_weight, cotangent=cotangent)


root_half = 0.7071067811865476
inv_root_tau = 0.3989422804014327


def gelu_pair(pre_act):
    cumul = 0.5 * (1.0 + jax.scipy.special.erf(pre_act * root_half))
    return pre_act * cumul, cumul + pre_act * jnp.exp(-0.5 * pre_act * pre_act) * inv_root_tau


def reference(tokens, width_index, up_weight, down_weight, cotangent):
    block_rows = math.gcd(TOKENS, 1024)
    block_count = TOKENS // block_rows
    table = jnp.array([FF // 8, FF // 4, FF // 2, FF], dtype=jnp.int32)
    limits = table[width_index].astype(jnp.int32)
    units = jnp.arange(FF, dtype=jnp.int32)
    token_blocks = tokens.reshape(block_count, block_rows, D)
    grad_blocks = cotangent.reshape(block_count, block_rows, D)
    limit_blocks = limits.reshape(block_count, block_rows)

    def one_block(carry, inputs):
        grad_up, grad_down = carry
        token_rows, grad_rows, limit_rows = inputs
        keep_mask = units[None, :] < limit_rows[:, None]
        pre_act = jnp.dot(token_rows, up_weight, preferred_element_type=jnp.float32)
        act_value, act_slope = gelu_pair(pre_act)
        hidden = jnp.where(keep_mask, act_value, 0.0).astype(jnp.bfloat16)
        mixed = jnp.dot(hidden, down_weight, preferred_element_type=jnp.float32).astype(jnp.bfloat16)
        grad_hidden = jnp.dot(grad_rows, down_weight.T, preferred_element_type=jnp.float32)
        grad_pre = jnp.where(keep_mask, grad_hidden * act_slope, 0.0).astype(jnp.bfloat16)
        grad_tokens = jnp.dot(grad_pre, up_weight.T, preferred_element_type=jnp.float32).astype(jnp.bfloat16)
        grad_up = grad_up + jnp.dot(token_rows.T, grad_pre, preferred_element_type=jnp.float32)
        grad_down = grad_down + jnp.dot(hidden.T, grad_rows, preferred_element_type=jnp.float32)
        return (grad_up, grad_down), (mixed, grad_tokens)

    start = (jnp.zeros((D, FF), jnp.float32), jnp.zeros((FF, D), jnp.float32))
    (grad_up, grad_down), (mixed, grad_tokens) = lax.scan(one_block, start, (token_blocks, grad_blocks, limit_blocks))
    return mixed.reshape(TOKENS, D), grad_tokens.reshape(TOKENS, D), grad_up, grad_down
```

```python
import jax
import jax.numpy as jnp
from jax import lax
from jax.experimental import pallas as pl
from jax.experimental.pallas import tpu as pltpu
from jax.sharding import PartitionSpec as P

root_half = 0.7071067811865476
inv_root_tau = 0.3989422804014327
F32 = jnp.float32
BF16 = jnp.bfloat16
MESH = pl.DeviceIdType.MESH

ROWS = 512
COLS = 256
D = 1024
UNITS = 1024
NZ, NY = 8, 4
TILE = 256
N_SEM = 128

NT = (((1,), (1,)), ((), ()))
TN = (((0,), (0,)), ((), ()))


def gelu_pair(pre_act):
    cumul = 0.5 * (1.0 + lax.erf(pre_act * root_half))
    return (pre_act * cumul, cumul + pre_act * jnp.exp(-0.5 * pre_act * pre_act) * inv_root_tau)


def kernel(
    tok_ref, wid_ref, up_ref, down_ref, cot_ref,
    mixed_ref, gtok_ref, gup_ref, gdown_ref,
    uf, vf, xg, hbuf, pbuf, so, ro, fo, perm, permt,
    gsend, grecv, lane,
    sv, rv, su0, ru0, su1, ru1, suz, ruz, svy0, rvy0, svy1, rvy1, uy, vz,
    ssem, rsem,
):
    hid = lax.axis_index("hid")
    tok = lax.axis_index("tok")
    c = lax.rem(tok, 2)
    y = lax.rem(lax.div(tok, 2), NY)
    z = lax.div(tok, 2 * NY)

    def zmod(v):
        return lax.rem(v + 2 * NZ, NZ)

    def ymod(v):
        return lax.rem(v + 2 * NY, NY)

    def at(zz, yy, cc):
        return {"tok": (zz * NY + yy) * 2 + cc}

    zp, zm = at(zmod(z + 1), y, c), at(zmod(z - 1), y, c)
    yp, ym = at(z, ymod(y + 1), c), at(z, ymod(y - 1), c)
    mate = at(z, y, 1 - c)
    near = (zp, zm, yp, ym, mate)
    xs = [{"hid": lax.rem(hid + k, 4)} for k in (1, 2, 3)]

    slots = {}
    sent = []

    def msg(key, src, dst, dev):
        if key not in slots:
            slots[key] = len(slots)
        i = slots[key]
        return pltpu.make_async_remote_copy(
            src_ref=src, dst_ref=dst, send_sem=ssem.at[i], recv_sem=rsem.at[i],
            device_id=dev, device_id_type=MESH,
        )

    def send(key, src, dst, dev, plane=None, again=None):
        msg(key, src, dst, dev).start()
        sent.append((key, again or (lambda: src), plane))

    def recv(key, dst):
        msg(key, dst, dst, mate).wait_recv()

    barrier = pltpu.get_barrier_semaphore()
    for dev in near + tuple(xs):
        pl.semaphore_signal(barrier, inc=1, device_id=dev, device_id_type=MESH)

    uf[z, y, c] = up_ref[...]
    vf[z, y, c] = down_ref[...]

    pl.semaphore_wait(barrier, len(near) + len(xs))

    y1, y3, y2 = ymod(y + 1), ymod(y - 1), ymod(y + 2)

    def u_z(direction, s):
        zz = zmod(z - s) if direction == 0 else zmod(z + s)
        send(("uz", direction, s), uf.at[zz, y, c], uf.at[zz, y, c], zp if direction == 0 else zm)

    def u_z_recv(direction, s):
        recv(("uz", direction, s), uf.at[z, y, c])

    def u_y(i, zz):
        for k, dev in ((0, yp), (1, ym)):
            send(("uy", i, k), uf.at[zz, y, c], uf.at[zz, y, c], dev)

    def u_y_recv(i, zz):
        recv(("uy", i, 0), uf.at[zz, y3, c])
        recv(("uy", i, 1), uf.at[zz, y1, c])
        if i % 2 == 0:
            send(("uyf", i), uf.at[zz, y3, c], uf.at[zz, y3, c], yp)
        else:
            send(("uyf", i), uf.at[zz, y1, c], uf.at[zz, y1, c], ym)

    def v_z(direction, half, s):
        zz = zmod(z - s) if direction == 0 else zmod(z + s)
        ref = vf.at[zz, pl.ds(2 * half, 2), c]
        send(("vz", direction, half, s), ref, ref, zp if direction == 0 else zm)

    def v_z_recv(direction, half, s):
        recv(("vz", direction, half, s), vf.at[z, pl.ds(2 * half, 2), c])

    order = [(None, 0), (0, 0), (1, 0), (0, 1), (1, 1), (0, 2), (1, 2), (0, 3)]
    z_of = [z] + [zmod(z - s - 1) if d == 0 else zmod(z + s + 1) for d, s in order[1:]]

    send(("vy", 0), vf.at[z, y, c], vf.at[z, y, c], yp)
    send(("vy", 1), vf.at[z, y, c], vf.at[z, y, c], ym)
    u_z(0, 0)
    u_z(1, 0)
    u_y(0, z)

    wid = wid_ref[...]
    level = lax.broadcasted_iota(jnp.int32, (8, ROWS), 0)
    ind = (jnp.broadcast_to(wid, (8, ROWS)) == level).astype(F32)
    ind16 = ind.astype(BF16)
    ia = lax.broadcasted_iota(jnp.int32, (ROWS, ROWS), 0)
    ib = lax.broadcasted_iota(jnp.int32, (ROWS, ROWS), 1)
    above = (ia < ib).astype(F32).astype(BF16)
    below = (ib < ia).astype(F32).astype(BF16)
    eye = (ia == ib).astype(F32).astype(BF16)
    counts = jnp.sum(ind, axis=1, keepdims=True)
    wider = [
        sum([counts[k:k + 1] for k in range(lo, 4)], jnp.zeros((1, 1), F32)) for lo in range(5)
    ]
    pre_row = jnp.dot(ind16, above, preferred_element_type=F32)
    pre_col = lax.dot_general(below, ind16, NT, preferred_element_type=F32)
    ind_col = lax.dot_general(eye, ind16, NT, preferred_element_type=F32)
    rank_row = sum([ind[k:k + 1] * (pre_row[k:k + 1] + wider[k + 1]) for k in range(4)])
    rank_col = sum(
        [ind_col[:, k:k + 1] * (pre_col[:, k:k + 1] + wider[k + 1]) for k in range(4)]
    )
    perm[...] = (ia == rank_row.astype(jnp.int32)).astype(F32).astype(BF16)
    permt[...] = (ib == rank_col.astype(jnp.int32)).astype(F32).astype(BF16)
    mine = pl.ds(pl.multiple_of(hid * COLS, COLS), COLS)
    for a, ref in ((0, tok_ref), (1, cot_ref)):
        xg[a, :, mine] = jnp.dot(perm[...], ref[...], preferred_element_type=F32).astype(BF16)

    def xpart(h, lo, hi):
        return xg.at[:, pl.ds(lo, hi - lo), pl.ds(h * COLS, COLS)]

    def xsend(src, dst, h, lo, hi):
        part = xpart(h, lo, hi)
        send(("x", src, dst, h, lo), part, part, xs[(dst - src) % 4 - 1], src,
             lambda: xpart(h, lo, hi))

    def xrecv(src, dst, h, lo, hi):
        recv(("x", src, dst, h, lo), xpart(h, lo, hi))

    @pl.when(hid == 2)
    def _():
        xsend(2, 1, 2, 0, 128)
        xsend(2, 3, 2, 128, 256)
        xsend(2, 3, 2, 0, 64)
        xsend(2, 1, 2, 256, 384)
        xsend(2, 3, 2, 384, 512)

    @pl.when(hid == 1)
    def _():
        xsend(1, 0, 1, 0, 256)
        xsend(1, 2, 1, 0, 64)
        xsend(1, 3, 1, 0, 64)
        xsend(1, 0, 1, 256, 512)

    @pl.when(hid == 3)
    def _():
        xsend(3, 0, 3, 0, 256)
        xsend(3, 2, 3, 0, 64)
        xsend(3, 1, 3, 0, 128)
        xsend(3, 0, 3, 256, 512)

    @pl.when(hid == 0)
    def _():
        xsend(0, 1, 0, 0, 128)
        xsend(0, 3, 0, 0, 64)
        xsend(0, 2, 0, 0, 64)

    def forward_tokens(part):
        @pl.when(hid == 1)
        def _():
            xrecv(2, 1, 2, 256 * part, 256 * part + 128)
            xsend(1, 0, 2, 256 * part, 256 * part + 128)

        @pl.when(hid == 3)
        def _():
            xrecv(2, 3, 2, 256 * part + 128, 256 * part + 256)
            xsend(3, 0, 2, 256 * part + 128, 256 * part + 256)

    recv(("vy", 0), vf.at[z, y3, c])
    send(("vyf", 0), vf.at[z, y3, c, :, pl.ds(0, 512)], vf.at[z, y3, c, :, pl.ds(0, 512)], yp)
    recv(("vy", 1), vf.at[z, y1, c])
    send(("vyf", 1), vf.at[z, y1, c, :, pl.ds(512, 512)], vf.at[z, y1, c, :, pl.ds(512, 512)], ym)
    for i in (1, 2):
        u_z_recv(*order[i])
        u_z(order[i][0], 1)
        u_y(i, z_of[i])
    recv(("vyf", 0), vf.at[z, y2, c, :, pl.ds(0, 512)])
    recv(("vyf", 1), vf.at[z, y2, c, :, pl.ds(512, 512)])
    for half in (0, 1):
        for direction in (0, 1):
            v_z(direction, half, 0)
    send(("vc", 0), vf.at[z, :, c], vf.at[z, :, c], mate)
    u_y_recv(0, z)
    forward_tokens(0)
    for i in (3, 4):
        u_z_recv(*order[i])
        if order[i][0] == 0 or order[i][1] < 2:
            u_z(order[i][0], 2)
        u_y(i, z_of[i])
    u_y_recv(1, z_of[1])
    u_y_recv(2, z_of[2])

    def v_hop(s):
        for half in (0, 1):
            for direction in (0, 1):
                last = 3 if half == direction else 2
                if s > last:
                    continue
                v_z_recv(direction, half, s)
                if s < last:
                    v_z(direction, half, s + 1)
        if s < 3:
            for k, zz in ((0, zmod(z - s - 1)), (1, zmod(z + s + 1))):
                send(("vc", 1 + 2 * s + k), vf.at[zz, :, c], vf.at[zz, :, c], mate)
        else:
            zz = zmod(z + 4)
            send(("vc", 7), vf.at[zz, :, c], vf.at[zz, :, c], mate)

    v_hop(0)
    forward_tokens(1)
    for i in (5, 6):
        u_z_recv(*order[i])
        if order[i][0] == 0:
            u_z(0, 3)
        u_y(i, z_of[i])
    u_y_recv(3, z_of[3])
    u_y_recv(4, z_of[4])
    u_z_recv(0, 3)
    u_y(7, z_of[7])
    v_hop(1)
    send(("uc", 0), uf.at[:, y, c], uf.at[:, y, c], mate)
    u_y_recv(5, z_of[5])
    u_y_recv(6, z_of[6])
    u_y_recv(7, z_of[7])
    send(("uc", 1), uf.at[:, y1, c], uf.at[:, y1, c], mate)
    send(("uc", 2), uf.at[:, y3, c], uf.at[:, y3, c], mate)
    v_hop(2)
    v_hop(3)
    for i in range(8):
        recv(("uyf", i), uf.at[z, y2, c])
    send(("uc", 3), uf.at[:, y2, c], uf.at[:, y2, c], mate)
    for i in range(4):
        recv(("uc", i), uf.at[:, y, 1 - c])
    for i in range(8):
        recv(("vc", i), vf.at[z, :, 1 - c])

    def units(lo_row, n_row, lo_tile, hi_tile, count):
        rows = pl.ds(lo_row, n_row)

        def body(j, carry):
            cols = pl.ds(pl.multiple_of(j * TILE, TILE), TILE)
            u = uf[:, :, :, :, cols].reshape(D, TILE)
            v = vf[:, :, :, :, cols].reshape(D, TILE)
            pre = jnp.dot(xg[0, rows, :], u, preferred_element_type=F32)
            gh = jnp.dot(xg[1, rows, :], v, preferred_element_type=F32)
            act, slope = gelu_pair(pre)
            pg = gh * slope
            if count is not None:
                row = lax.broadcasted_iota(jnp.int32, (n_row, TILE), 0).astype(F32) + lo_row
                keep = row < count
                act = jnp.where(keep, act, 0.0)
                pg = jnp.where(keep, pg, 0.0)
            hbuf[rows, cols] = act.astype(BF16)
            pbuf[rows, cols] = pg.astype(BF16)
            return carry

        lax.fori_loop(lo_tile, hi_tile, body, 0)

    def outputs(plane, d, lo_row, n_row, n_unit):
        rows = pl.ds(lo_row, n_row)
        for a, val, w in ((0, hbuf, vf), (1, pbuf, uf)):
            wt = w[2 * d:2 * d + 2].reshape(COLS, UNITS)[:, :n_unit]
            out = lax.dot_general(val[rows, :n_unit], wt, NT, preferred_element_type=F32)
            if d == plane:
                ro[plane, a, rows, :] = out.astype(BF16)
            else:
                so[d, a, rows, :] = out.astype(BF16)

    def osend(src, dst, d, lo, hi, via=False):
        part = so.at[d, :, pl.ds(lo, hi - lo), :]
        to = fo.at[:, pl.ds(lo, hi - lo), :] if via else ro.at[src, :, pl.ds(lo, hi - lo), :]
        send(("o", src, dst, d, lo), part, to, xs[(dst - src) % 4 - 1], src,
             lambda: so.at[d, :, pl.ds(lo, hi - lo), :])

    def orecv(src, lo, hi, dst):
        recv(("o", src, dst, dst, lo), ro.at[src, :, pl.ds(lo, hi - lo), :])

    def grads(full, n_row):
        for a, val in ((1, hbuf), (0, pbuf)):
            def body(dt, carry):
                cols = pl.ds(pl.multiple_of(dt * COLS, COLS), COLS)
                if full:
                    left = lax.dot_general(
                        xg[a, :, cols], val[:, :512], TN, preferred_element_type=F32)
                    right = lax.dot_general(
                        xg[a, :256, cols], val[:256, 512:], TN, preferred_element_type=F32)
                    g = jnp.concatenate([left, right], axis=1)
                else:
                    g = lax.dot_general(
                        xg[a, :n_row, cols], val[:n_row, :], TN, preferred_element_type=F32)
                g = g.reshape(2, NY, 2, 16, UNITS)
                lane[a, pl.ds(2 * dt, 2)] = jnp.where(c == 0, g[:, :, 0], g[:, :, 1])
                gsend[a, pl.ds(2 * dt, 2)] = jnp.where(c == 0, g[:, :, 1], g[:, :, 0]).astype(BF16)
                return carry

            lax.fori_loop(0, 4, body, 0)

    @pl.when(hid == 0)
    def _():
        xrecv(1, 0, 1, 0, 256)
        xrecv(3, 0, 3, 0, 256)
        xrecv(1, 0, 2, 0, 128)
        xrecv(3, 0, 2, 128, 256)
        units(0, 256, 0, 2, None)
        units(0, 256, 2, 4, wider[1])
        for d in (2, 1, 3, 0):
            outputs(0, d, 0, 256, 1024)
            if d == 2:
                osend(0, 1, 2, 0, 128, True)
                osend(0, 3, 2, 128, 256, True)
            elif d:
                osend(0, d, d, 0, 256)
        xrecv(1, 0, 1, 256, 512)
        xrecv(3, 0, 3, 256, 512)
        xrecv(1, 0, 2, 256, 384)
        xrecv(3, 0, 2, 384, 512)
        units(256, 256, 0, 2, None)
        for d in (2, 1, 3, 0):
            outputs(0, d, 256, 256, 512)
            if d == 2:
                osend(0, 1, 2, 256, 384, True)
                osend(0, 3, 2, 384, 512, True)
            elif d:
                osend(0, d, d, 256, 512)
        grads(True, 512)

    @pl.when(hid == 1)
    def _():
        xrecv(0, 1, 0, 0, 128)
        xrecv(3, 1, 3, 0, 128)
        units(0, 128, 0, 4, wider[2])
        for d in (0, 3, 2, 1):
            outputs(1, d, 0, 128, 1024)
            if d != 1:
                osend(1, d, d, 0, 128)
        grads(False, 128)

    @pl.when(hid == 2)
    def _():
        for s in (0, 1, 3):
            xrecv(s, 2, s, 0, 64)
        units(0, 64, 0, 4, wider[3])
        for d in (0, 1, 3, 2):
            outputs(2, d, 0, 64, 1024)
            if d != 2:
                osend(2, d, d, 0, 64)
        grads(False, 64)

    @pl.when(hid == 3)
    def _():
        for s in (0, 1, 2):
            xrecv(s, 3, s, 0, 64)
        units(0, 64, 0, 4, wider[3])
        for d in (1, 0, 2, 3):
            outputs(3, d, 0, 64, 1024)
            if d != 3:
                osend(3, d, d, 0, 64)
        grads(False, 64)

    for a in (1, 0):
        send(("gc", a), gsend.at[a], grecv.at[a], mate)

    def forward_outputs(part):
        for plane, lo in ((1, 256 * part), (3, 256 * part + 128)):
            @pl.when(hid == plane)
            def _():
                recv(("o", 0, plane, 2, lo), fo.at[:, pl.ds(lo, 128), :])
                send(("of", plane, lo), fo.at[:, pl.ds(lo, 128), :],
                     ro.at[0, :, pl.ds(lo, 128), :], xs[(2 - plane) % 4 - 1], plane,
                     lambda lo=lo: fo.at[:, pl.ds(lo, 128), :])

    def total(a, zz, yy):
        return lane[a, zz, yy] + grecv[a, zz, yy].astype(F32)

    def v_step(direction, s):
        zz = zmod(z + 4 - s) if direction == 0 else zmod(z - 4 + s)
        first, last = 2 * direction, 2 * direction + 2
        for yy in range(NY):
            if s == 0 and not first <= yy < last:
                continue
            val = total(1, zz, yy)
            if s > 1 or (s == 1 and first <= yy < last):
                val = val + rv[direction, s - 1, yy].astype(F32)
            sv[direction, s, yy] = val.astype(BF16)
        ys = pl.ds(first, 2) if s == 0 else pl.ds(0, NY)
        send(("v", direction, s), sv.at[direction, s, ys], rv.at[direction, s, ys],
             zp if direction == 0 else zm)

    def v_step_recv(direction, s):
        ys = pl.ds(2 * direction, 2) if s == 0 else pl.ds(0, NY)
        recv(("v", direction, s), rv.at[direction, s, ys])

    recv(("gc", 1), grecv.at[1])
    v_step(0, 0)
    v_step(1, 0)
    recv(("gc", 0), grecv.at[0])
    for k, dev in ((0, yp), (1, ym)):
        for i in range(4):
            su0[k, i] = total(0, 4 * k + i, y2).astype(BF16)
        send(("u0", k), su0.at[k], ru0.at[k], dev)
    forward_outputs(0)
    for direction in (0, 1):
        v_step_recv(direction, 0)
        v_step(direction, 1)
    for k, dev, yy in ((0, yp, y1), (1, ym, y3)):
        recv(("u0", k), ru0.at[k])
        for i in range(NZ):
            val = total(0, i, yy)
            if i // 4 == k:
                val = val + ru0[k, i % 4].astype(F32)
            su1[k, i] = val.astype(BF16)
        send(("u1", k), su1.at[k], ru1.at[k], dev)
    for s in (1, 2):
        for direction in (0, 1):
            v_step_recv(direction, s)
            v_step(direction, s + 1)
    forward_outputs(1)
    recv(("u1", 0), ru1.at[0])
    recv(("u1", 1), ru1.at[1])
    for i in range(NZ):
        uy[i] = total(0, i, y) + ru1[0, i].astype(F32) + ru1[1, i].astype(F32)

    def u_step(direction, s):
        zz = zmod(z + 4 - s) if direction == 0 else zmod(z - 3 + s)
        val = uy[zz]
        if s:
            val = val + ruz[direction, s - 1].astype(F32)
        suz[direction, s] = val.astype(BF16)
        send(("u", direction, s), suz.at[direction, s], ruz.at[direction, s],
             zp if direction == 0 else zm)

    def u_step_recv(direction, s):
        recv(("u", direction, s), ruz.at[direction, s])

    u_step(0, 0)
    u_step(1, 0)
    v_step_recv(0, 3)
    v_step_recv(1, 3)
    for yy in range(NY):
        vz[yy] = total(1, z, yy) + rv[0, 3, yy].astype(F32) + rv[1, 3, yy].astype(F32)
    for k, dev in ((0, yp), (1, ym)):
        svy0[k] = vz[y2, :, 512 * k:512 * k + 512].astype(BF16)
        send(("vy0", k), svy0.at[k], rvy0.at[k], dev)
    u_step_recv(0, 0)
    u_step(0, 1)
    u_step_recv(1, 0)
    u_step(1, 1)
    for k, dev, yy in ((0, yp, y1), (1, ym, y3)):
        recv(("vy0", k), rvy0.at[k])
        own = vz[yy]
        got = rvy0[k].astype(F32)
        if k == 0:
            val = jnp.concatenate([own[:, :512] + got, own[:, 512:]], axis=1)
        else:
            val = jnp.concatenate([own[:, :512], own[:, 512:] + got], axis=1)
        svy1[k] = val.astype(BF16)
        send(("vy1", k), svy1.at[k], rvy1.at[k], dev)
    u_step_recv(0, 1)
    u_step(0, 2)
    u_step_recv(1, 1)
    u_step(1, 2)
    u_step_recv(0, 2)
    u_step(0, 3)
    for k in (0, 1):
        recv(("vy1", k), rvy1.at[k])
    gdown_ref[...] = vz[y] + rvy1[0].astype(F32) + rvy1[1].astype(F32)

    @pl.when(hid == 0)
    def _():
        orecv(1, 0, 128, 0)
        orecv(2, 0, 64, 0)
        orecv(3, 0, 64, 0)

    for plane in (1, 3):
        @pl.when(hid == plane)
        def _():
            orecv(0, 0, 256, plane)
            orecv(0, 256, 512, plane)
            for s, n in ((1, 128), (2, 64), (3, 64)):
                if s != plane:
                    orecv(s, 0, n, plane)

    @pl.when(hid == 2)
    def _():
        for plane, lo in ((1, 0), (3, 128), (1, 256), (3, 384)):
            recv(("of", plane, lo), ro.at[0, :, pl.ds(lo, 128), :])
        orecv(1, 0, 128, 2)
        orecv(3, 0, 64, 2)

    for a, ref in ((0, mixed_ref), (1, gtok_ref)):
        top = ro[0, a, 0:128].astype(F32) + ro[1, a, 0:128].astype(F32)
        wide = top[:64] + ro[2, a, 0:64].astype(F32) + ro[3, a, 0:64].astype(F32)
        ro[0, a, 0:128] = jnp.concatenate([wide, top[64:]], axis=0).astype(BF16)
        ref[...] = jnp.dot(permt[...], ro[0, a], preferred_element_type=F32).astype(BF16)

    u_step_recv(1, 2)
    u_step_recv(0, 3)
    gup_ref[...] = uy[z] + ruz[0, 3].astype(F32) + ruz[1, 2].astype(F32)

    def left(which):
        for key, src, plane in sent:
            if plane == which:
                msg(key, src(), src(), mate).wait_send()

    left(None)
    for plane in range(4):
        @pl.when(hid == plane)
        def _():
            left(plane)
    assert len(slots) <= N_SEM, len(slots)


def per_device(tokens, width_index, up_weight, down_weight, cotangent):
    vm = pl.BlockSpec(memory_space=pltpu.VMEM)
    block = (16, UNITS)

    def buf(*shape):
        return pltpu.VMEM(shape, BF16)

    mixed, gtok, gup, gdown = pl.pallas_call(
        kernel,
        out_shape=(
            jax.ShapeDtypeStruct((ROWS, COLS), BF16),
            jax.ShapeDtypeStruct((ROWS, COLS), BF16),
            jax.ShapeDtypeStruct(block, F32),
            jax.ShapeDtypeStruct(block, F32),
        ),
        in_specs=[vm] * 5,
        out_specs=(vm,) * 4,
        scratch_shapes=[
            buf(NZ, NY, 2, *block), buf(NZ, NY, 2, *block),
            buf(2, ROWS, D), buf(ROWS, UNITS), buf(ROWS, UNITS),
            buf(4, 2, ROWS, COLS), buf(4, 2, ROWS, COLS), buf(2, ROWS, COLS),
            buf(ROWS, ROWS), buf(ROWS, ROWS),
            buf(2, NZ, NY, *block), buf(2, NZ, NY, *block),
            pltpu.VMEM((2, NZ, NY, *block), F32),
            buf(2, 4, NY, *block), buf(2, 4, NY, *block),
            buf(2, 4, *block), buf(2, 4, *block),
            buf(2, NZ, *block), buf(2, NZ, *block),
            buf(2, 4, *block), buf(2, 4, *block),
            buf(2, 16, 512), buf(2, 16, 512),
            buf(2, *block), buf(2, *block),
            pltpu.VMEM((NZ, *block), F32), pltpu.VMEM((NY, *block), F32),
            pltpu.SemaphoreType.DMA((N_SEM,)), pltpu.SemaphoreType.DMA((N_SEM,)),
        ],
        compiler_params=pltpu.CompilerParams(
            collective_id=0, has_side_effects=True, vmem_limit_bytes=56 * 1024 * 1024,
        ),
    )(tokens, width_index.reshape(1, ROWS), up_weight, down_weight.T, cotangent)
    return mixed, gtok, gup, gdown.T


def solution(mesh):
    placed = (P("tok", "hid"), P("tok"), P("tok", "hid"), P("hid", "tok"), P("tok", "hid"))
    return jax.shard_map(
        per_device,
        mesh=mesh,
        in_specs=placed,
        out_specs=(P("tok", "hid"), P("tok", "hid"), P("tok", "hid"), P("hid", "tok")),
        check_vma=False,
    )
```

```python
import jax
import jax.numpy as jnp
from jax import lax
from jax.experimental import pallas as pl
from jax.experimental.pallas import tpu as pltpu
from jax.sharding import PartitionSpec as P

root_half = 0.7071067811865476
inv_root_tau = 0.3989422804014327
F32 = jnp.float32
BF16 = jnp.bfloat16
MESH = pl.DeviceIdType.MESH

ROWS = 512
COLS = 256
D = 1024
UNITS = 1024
NZ, NY = 8, 4
TILE = 256
N_SEM = 224

NT = (((1,), (1,)), ((), ()))
TN = (((0,), (0,)), ((), ()))


def gelu_pair(pre_act):
    cumul = 0.5 * (1.0 + lax.erf(pre_act * root_half))
    return (pre_act * cumul, cumul + pre_act * jnp.exp(-0.5 * pre_act * pre_act) * inv_root_tau)


def kernel(
    tok_ref, wid_ref, up_ref, down_ref, cot_ref,
    mixed_ref, gtok_ref, gup_ref, gdown_ref,
    uf, vf, xg, hbuf, pbuf, so, ro, fo, perm, permt,
    gsend, grecv, lane,
    sv, rv, su1, ru1, suz, ruz, svy, rvy, uy, vz,
    ssem, rsem,
):
    hid = lax.axis_index("hid")
    tok = lax.axis_index("tok")
    c = lax.rem(tok, 2)
    y = lax.rem(lax.div(tok, 2), NY)
    z = lax.div(tok, 2 * NY)

    def zmod(v):
        return lax.rem(v + 2 * NZ, NZ)

    def ymod(v):
        return lax.rem(v + 2 * NY, NY)

    def at(zz, yy, cc):
        return {"tok": (zz * NY + yy) * 2 + cc}

    zp, zm = at(zmod(z + 1), y, c), at(zmod(z - 1), y, c)
    mate = at(z, y, 1 - c)
    near = [at(zmod(z + k), y, c) for k in (1, -1, 2, -2, 3, -3, 4)]
    near += [at(z, ymod(y + r), c) for r in (1, 2, 3)] + [mate]
    xs = [{"hid": lax.rem(hid + k, 4)} for k in (1, 2, 3)]

    slots = {}
    sent = []

    def msg(key, src, dst, dev):
        if key not in slots:
            slots[key] = len(slots)
        i = slots[key]
        return pltpu.make_async_remote_copy(
            src_ref=src, dst_ref=dst, send_sem=ssem.at[i], recv_sem=rsem.at[i],
            device_id=dev, device_id_type=MESH,
        )

    def send(key, src, dst, dev, plane=None, again=None):
        msg(key, src, dst, dev).start()
        sent.append((key, again or (lambda: src), plane))

    def recv(key, dst):
        msg(key, dst, dst, mate).wait_recv()

    barrier = pltpu.get_barrier_semaphore()
    for dev in near + xs:
        pl.semaphore_signal(barrier, inc=1, device_id=dev, device_id_type=MESH)

    uf[z, y, c] = up_ref[...]
    vf[z, y, c] = down_ref[...]

    pl.semaphore_wait(barrier, len(near) + len(xs))

    def peer_y(r):
        return ymod(y + r)

    def u_share(k):
        zz = zmod(z + k)
        for r in (1, 3, 2):
            ref = uf.at[zz, y, c]
            send(("uy", k, r), ref, ref, at(z, peer_y(r), c))

    def u_direct(k):
        ref = uf.at[z, y, c]
        send(("uz", k), ref, ref, at(zmod(z + k), y, c))

    def u_pass(k, step):
        ref = uf.at[zmod(z + k), y, c]
        send(("uz", step - k), ref, ref, at(zmod(z + step), y, c))

    def u_recv(k):
        recv(("uz", -k if k != 4 else 4), uf.at[z, y, c])

    def u_group(k):
        for r in (1, 3, 2):
            recv(("uy", k, r), uf.at[z, y, c])
        zz = zmod(z + k)
        send(("uc", k), uf.at[zz, :, c], uf.at[zz, :, c], mate)

    def hops(r, d):
        return 4 if (r < 2) == (d == 0) else 3

    def v_send(r, d, s):
        zz = zmod(z - s) if d == 0 else zmod(z + s)
        ref = vf.at[zz, peer_y(r), c]
        send(("vz", r, d, s), ref, ref, zp if d == 0 else zm)

    def v_recv(r, d, s):
        if s < hops(r, d):
            recv(("vz", r, d, s), vf.at[z, y, c])
            if s + 1 < hops(r, d):
                v_send(r, d, s + 1)

    def v_mate(k):
        zz = zmod(z + k)
        send(("vc", k), vf.at[zz, :, c], vf.at[zz, :, c], mate)

    own_v = vf.at[z, y, c]
    for r in (1, 3, 2):
        send(("vy", r), own_v, own_v, at(z, peer_y(r), c))
    v_send(0, 0, 0)
    v_send(0, 1, 0)
    u_direct(1)
    u_direct(-1)
    u_share(0)
    u_direct(2)
    u_direct(-2)
    u_direct(4)

    wid = wid_ref[...]
    level = lax.broadcasted_iota(jnp.int32, (8, ROWS), 0)
    ind = (jnp.broadcast_to(wid, (8, ROWS)) == level).astype(F32)
    ind16 = ind.astype(BF16)
    ia = lax.broadcasted_iota(jnp.int32, (ROWS, ROWS), 0)
    ib = lax.broadcasted_iota(jnp.int32, (ROWS, ROWS), 1)
    above = (ia < ib).astype(F32).astype(BF16)
    below = (ib < ia).astype(F32).astype(BF16)
    eye = (ia == ib).astype(F32).astype(BF16)
    counts = jnp.sum(ind, axis=1, keepdims=True)
    wider = [
        sum([counts[k:k + 1] for k in range(lo, 4)], jnp.zeros((1, 1), F32)) for lo in range(5)
    ]
    pre_row = jnp.dot(ind16, above, preferred_element_type=F32)
    pre_col = lax.dot_general(below, ind16, NT, preferred_element_type=F32)
    ind_col = lax.dot_general(eye, ind16, NT, preferred_element_type=F32)
    rank_row = sum([ind[k:k + 1] * (pre_row[k:k + 1] + wider[k + 1]) for k in range(4)])
    rank_col = sum(
        [ind_col[:, k:k + 1] * (pre_col[:, k:k + 1] + wider[k + 1]) for k in range(4)]
    )
    perm[...] = (ia == rank_row.astype(jnp.int32)).astype(F32).astype(BF16)
    permt[...] = (ib == rank_col.astype(jnp.int32)).astype(F32).astype(BF16)
    mine = pl.ds(pl.multiple_of(hid * COLS, COLS), COLS)
    for a, ref in ((0, tok_ref), (1, cot_ref)):
        xg[a, :, mine] = jnp.dot(perm[...], ref[...], preferred_element_type=F32).astype(BF16)

    def xpart(h, lo, hi):
        return xg.at[:, pl.ds(lo, hi - lo), pl.ds(h * COLS, COLS)]

    def xsend(src, dst, h, lo, hi):
        part = xpart(h, lo, hi)
        send(("x", src, dst, h, lo), part, part, xs[(dst - src) % 4 - 1], src,
             lambda: xpart(h, lo, hi))

    def xrecv(src, dst, h, lo, hi):
        recv(("x", src, dst, h, lo), xpart(h, lo, hi))

    @pl.when(hid == 2)
    def _():
        xsend(2, 1, 2, 0, 128)
        xsend(2, 3, 2, 128, 256)
        xsend(2, 3, 2, 0, 64)
        xsend(2, 1, 2, 256, 384)
        xsend(2, 3, 2, 384, 512)

    @pl.when(hid == 1)
    def _():
        xsend(1, 0, 1, 0, 256)
        xsend(1, 2, 1, 0, 64)
        xsend(1, 3, 1, 0, 64)
        xsend(1, 0, 1, 256, 512)

    @pl.when(hid == 3)
    def _():
        xsend(3, 0, 3, 0, 256)
        xsend(3, 2, 3, 0, 64)
        xsend(3, 1, 3, 0, 128)
        xsend(3, 0, 3, 256, 512)

    @pl.when(hid == 0)
    def _():
        xsend(0, 1, 0, 0, 128)
        xsend(0, 3, 0, 0, 64)
        xsend(0, 2, 0, 0, 64)

    def forward_tokens(part):
        @pl.when(hid == 1)
        def _():
            xrecv(2, 1, 2, 256 * part, 256 * part + 128)
            xsend(1, 0, 2, 256 * part, 256 * part + 128)

        @pl.when(hid == 3)
        def _():
            xrecv(2, 3, 2, 256 * part + 128, 256 * part + 256)
            xsend(3, 0, 2, 256 * part + 128, 256 * part + 256)

    for r in (3, 1, 2):
        recv(("vy", (4 - r) % 4), own_v)
        v_send(r, 0, 0)
        v_send(r, 1, 0)
    for k in (1, -1):
        u_recv(k)
        u_share(k)
    v_recv(0, 0, 0)
    v_recv(0, 1, 0)
    for k in (2, -2):
        u_recv(k)
        u_pass(k, -1 if k > 0 else 1)
        u_share(k)
    u_recv(4)
    u_share(4)
    forward_tokens(0)
    for r in (3, 1, 2):
        v_recv(r, 0, 0)
        v_recv(r, 1, 0)
    v_mate(0)
    v_mate(-1)
    v_mate(1)
    for k in (3, -3):
        u_recv(k)
        u_share(k)
    u_group(0)
    for r in range(4):
        v_recv(r, 0, 1)
        v_recv(r, 1, 1)
    v_mate(-2)
    v_mate(2)
    u_group(1)
    u_group(-1)
    forward_tokens(1)
    for r in range(4):
        v_recv(r, 0, 2)
        v_recv(r, 1, 2)
    v_mate(-3)
    v_mate(3)
    u_group(2)
    u_group(-2)
    u_group(4)
    for r in range(4):
        v_recv(r, 0, 3)
        v_recv(r, 1, 3)
    v_mate(4)
    u_group(3)
    u_group(-3)
    for k in (0, -1, 1, -2, 2, -3, 3, 4):
        recv(("uc", k), uf.at[z, :, 1 - c])
        recv(("vc", k), vf.at[z, :, 1 - c])

    def units(lo_row, n_row, lo_tile, hi_tile, count):
        rows = pl.ds(lo_row, n_row)

        def body(j, carry):
            cols = pl.ds(pl.multiple_of(j * TILE, TILE), TILE)
            u = uf[:, :, :, :, cols].reshape(D, TILE)
            v = vf[:, :, :, :, cols].reshape(D, TILE)
            pre = jnp.dot(xg[0, rows, :], u, preferred_element_type=F32)
            gh = jnp.dot(xg[1, rows, :], v, preferred_element_type=F32)
            act, slope = gelu_pair(pre)
            pg = gh * slope
            if count is not None:
                row = lax.broadcasted_iota(jnp.int32, (n_row, TILE), 0).astype(F32) + lo_row
                keep = row < count
                act = jnp.where(keep, act, 0.0)
                pg = jnp.where(keep, pg, 0.0)
            hbuf[rows, cols] = act.astype(BF16)
            pbuf[rows, cols] = pg.astype(BF16)
            return carry

        lax.fori_loop(lo_tile, hi_tile, body, 0)

    def outputs(plane, d, lo_row, n_row, n_unit):
        rows = pl.ds(lo_row, n_row)
        for a, val, w in ((0, hbuf, vf), (1, pbuf, uf)):
            wt = w[2 * d:2 * d + 2].reshape(COLS, UNITS)[:, :n_unit]
            out = lax.dot_general(val[rows, :n_unit], wt, NT, preferred_element_type=F32)
            if d == plane:
                ro[plane, a, rows, :] = out.astype(BF16)
            else:
                so[d, a, rows, :] = out.astype(BF16)

    def osend(src, dst, d, lo, hi, via=False):
        part = so.at[d, :, pl.ds(lo, hi - lo), :]
        to = fo.at[:, pl.ds(lo, hi - lo), :] if via else ro.at[src, :, pl.ds(lo, hi - lo), :]
        send(("o", src, dst, d, lo), part, to, xs[(dst - src) % 4 - 1], src,
             lambda: so.at[d, :, pl.ds(lo, hi - lo), :])

    def orecv(src, lo, hi, dst):
        recv(("o", src, dst, dst, lo), ro.at[src, :, pl.ds(lo, hi - lo), :])

    def tile(i):
        return lax.rem(lax.div(z, 2) + (2, 1, 3, 0)[i], 4)

    def grads(plane, n_row):
        for i in range(4):
            dt = tile(i)
            cols = pl.ds(pl.multiple_of(dt * COLS, COLS), COLS)
            zs = pl.ds(2 * dt, 2)
            for a, val in ((1, hbuf), (0, pbuf)):
                if plane == 0:
                    left = lax.dot_general(
                        xg[a, :, cols], val[:, :512], TN, preferred_element_type=F32)
                    right = lax.dot_general(
                        xg[a, :256, cols], val[:256, 512:], TN, preferred_element_type=F32)
                    g = jnp.concatenate([left, right], axis=1)
                else:
                    g = lax.dot_general(
                        xg[a, :n_row, cols], val[:n_row, :], TN, preferred_element_type=F32)
                g = g.reshape(2, NY, 2, 16, UNITS)
                lane[a, zs] = jnp.where(c == 0, g[:, :, 0], g[:, :, 1])
                gsend[a, zs] = jnp.where(c == 0, g[:, :, 1], g[:, :, 0]).astype(BF16)
                send(("gc", a, i), gsend.at[a, zs], grecv.at[a, zs], mate, plane,
                     lambda: gsend.at[0, pl.ds(0, 2)])

    def mate_grads(a, tiles):
        for i in tiles:
            recv(("gc", a, i), grecv.at[a, pl.ds(0, 2)])

    @pl.when(hid == 0)
    def _():
        xrecv(1, 0, 1, 0, 256)
        xrecv(3, 0, 3, 0, 256)
        xrecv(1, 0, 2, 0, 128)
        xrecv(3, 0, 2, 128, 256)
        units(0, 256, 0, 2, None)
        units(0, 256, 2, 4, wider[1])
        for d in (2, 1, 3, 0):
            outputs(0, d, 0, 256, 1024)
            if d == 2:
                osend(0, 1, 2, 0, 128, True)
                osend(0, 3, 2, 128, 256, True)
            elif d:
                osend(0, d, d, 0, 256)
        xrecv(1, 0, 1, 256, 512)
        xrecv(3, 0, 3, 256, 512)
        xrecv(1, 0, 2, 256, 384)
        xrecv(3, 0, 2, 384, 512)
        units(256, 256, 0, 2, None)
        for d in (2, 1, 3, 0):
            outputs(0, d, 256, 256, 512)
            if d == 2:
                osend(0, 1, 2, 256, 384, True)
                osend(0, 3, 2, 384, 512, True)
            elif d:
                osend(0, d, d, 256, 512)
        grads(0, 512)

    @pl.when(hid == 1)
    def _():
        xrecv(0, 1, 0, 0, 128)
        xrecv(3, 1, 3, 0, 128)
        units(0, 128, 0, 4, wider[2])
        for d in (0, 3, 2, 1):
            outputs(1, d, 0, 128, 1024)
            if d != 1:
                osend(1, d, d, 0, 128)
        grads(1, 128)

    @pl.when(hid == 2)
    def _():
        for s in (0, 1, 3):
            xrecv(s, 2, s, 0, 64)
        units(0, 64, 0, 4, wider[3])
        for d in (0, 1, 3, 2):
            outputs(2, d, 0, 64, 1024)
            if d != 2:
                osend(2, d, d, 0, 64)
        grads(2, 64)

    @pl.when(hid == 3)
    def _():
        for s in (0, 1, 2):
            xrecv(s, 3, s, 0, 64)
        units(0, 64, 0, 4, wider[3])
        for d in (1, 0, 2, 3):
            outputs(3, d, 0, 64, 1024)
            if d != 3:
                osend(3, d, d, 0, 64)
        grads(3, 64)

    def forward_outputs(part):
        for plane, lo in ((1, 256 * part), (3, 256 * part + 128)):
            @pl.when(hid == plane)
            def _():
                recv(("o", 0, plane, 2, lo), fo.at[:, pl.ds(lo, 128), :])
                send(("of", plane, lo), fo.at[:, pl.ds(lo, 128), :],
                     ro.at[0, :, pl.ds(lo, 128), :], xs[(2 - plane) % 4 - 1], plane,
                     lambda lo=lo: fo.at[:, pl.ds(lo, 128), :])

    def total(a, zz, yy):
        return lane[a, zz, yy] + grecv[a, zz, yy].astype(F32)

    def ring_send(r, d, s):
        zz = zmod(z + 4 - s) if d == 0 else zmod(z - 4 + s)
        val = total(1, zz, peer_y(r))
        if s > 4 - hops(r, d):
            val = val + rv[d, s - 1, r].astype(F32)
        sv[d, s, r] = val.astype(BF16)
        send(("v", r, d, s), sv.at[d, s, r], rv.at[d, s, r], zp if d == 0 else zm)

    def ring_step(s):
        for r in range(4):
            for d in (0, 1):
                if s > 4 - hops(r, d):
                    recv(("v", r, d, s - 1), rv.at[d, s - 1, r])
                if s >= 4 - hops(r, d):
                    ring_send(r, d, s)

    def up_share(k):
        for r in (1, 3, 2):
            su1[k + 3, r] = total(0, zmod(z + k), peer_y(r)).astype(BF16)
            send(("uu", k, r), su1.at[k + 3, r], ru1.at[k + 3, r], at(z, peer_y(r), c))

    def up_sum(k):
        val = total(0, zmod(z + k), y)
        for r in (1, 3, 2):
            recv(("uu", k, r), ru1.at[k + 3, r])
            val = val + ru1[k + 3, r].astype(F32)
        return val

    def up_direct(k):
        suz[k + 3] = up_sum(k).astype(BF16)
        send(("uw", k), suz.at[k + 3], ruz.at[k + 3], at(zmod(z + k), y, c))

    mate_grads(1, (0,))
    ring_step(0)
    mate_grads(0, (0,))
    up_share(4)
    mate_grads(1, (1, 2))
    ring_step(1)
    mate_grads(0, (1, 2))
    for k in (3, -3, 2, -2):
        up_share(k)
    forward_outputs(0)
    mate_grads(1, (3,))
    ring_step(2)
    mate_grads(0, (3,))
    for k in (1, -1, 0):
        up_share(k)
    up_direct(4)
    up_direct(3)
    up_direct(-3)
    ring_step(3)
    forward_outputs(1)
    up_direct(2)
    up_direct(-2)
    up_direct(1)
    up_direct(-1)
    uy[...] = up_sum(0)
    for r in (1, 3, 2, 0):
        val = total(1, z, peer_y(r))
        for d in (0, 1):
            recv(("v", r, d, 3), rv.at[d, 3, r])
            val = val + rv[d, 3, r].astype(F32)
        if r:
            svy[r] = val.astype(BF16)
            send(("vw", r), svy.at[r], rvy.at[r], at(z, peer_y(r), c))
        else:
            vz[...] = val

    @pl.when(hid == 0)
    def _():
        orecv(1, 0, 128, 0)
        orecv(2, 0, 64, 0)
        orecv(3, 0, 64, 0)

    for plane in (1, 3):
        @pl.when(hid == plane)
        def _():
            orecv(0, 0, 256, plane)
            orecv(0, 256, 512, plane)
            for s, n in ((1, 128), (2, 64), (3, 64)):
                if s != plane:
                    orecv(s, 0, n, plane)

    @pl.when(hid == 2)
    def _():
        for plane, lo in ((1, 0), (3, 128), (1, 256), (3, 384)):
            recv(("of", plane, lo), ro.at[0, :, pl.ds(lo, 128), :])
        orecv(1, 0, 128, 2)
        orecv(3, 0, 64, 2)

    for a, ref in ((0, mixed_ref), (1, gtok_ref)):
        top = ro[0, a, 0:128].astype(F32) + ro[1, a, 0:128].astype(F32)
        wide = top[:64] + ro[2, a, 0:64].astype(F32) + ro[3, a, 0:64].astype(F32)
        ro[0, a, 0:128] = jnp.concatenate([wide, top[64:]], axis=0).astype(BF16)
        ref[...] = jnp.dot(permt[...], ro[0, a], preferred_element_type=F32).astype(BF16)

    val = vz[...]
    for r in (1, 3, 2):
        recv(("vw", r), rvy.at[r])
        val = val + rvy[r].astype(F32)
    gdown_ref[...] = val
    val = uy[...]
    for k in (4, 3, -3, 2, -2, 1, -1):
        recv(("uw", k), ruz.at[k + 3])
        val = val + ruz[k + 3].astype(F32)
    gup_ref[...] = val

    def left(which):
        for key, src, plane in sent:
            if plane == which:
                msg(key, src(), src(), mate).wait_send()

    left(None)
    for plane in range(4):
        @pl.when(hid == plane)
        def _():
            left(plane)
    assert len(slots) <= N_SEM, len(slots)


def per_device(tokens, width_index, up_weight, down_weight, cotangent):
    vm = pl.BlockSpec(memory_space=pltpu.VMEM)
    block = (16, UNITS)

    def buf(*shape):
        return pltpu.VMEM(shape, BF16)

    mixed, gtok, gup, gdown = pl.pallas_call(
        kernel,
        out_shape=(
            jax.ShapeDtypeStruct((ROWS, COLS), BF16),
            jax.ShapeDtypeStruct((ROWS, COLS), BF16),
            jax.ShapeDtypeStruct(block, F32),
            jax.ShapeDtypeStruct(block, F32),
        ),
        in_specs=[vm] * 5,
        out_specs=(vm,) * 4,
        scratch_shapes=[
            buf(NZ, NY, 2, *block), buf(NZ, NY, 2, *block),
            buf(2, ROWS, D), buf(ROWS, UNITS), buf(ROWS, UNITS),
            buf(4, 2, ROWS, COLS), buf(4, 2, ROWS, COLS), buf(2, ROWS, COLS),
            buf(ROWS, ROWS), buf(ROWS, ROWS),
            buf(2, NZ, NY, *block), buf(2, NZ, NY, *block),
            pltpu.VMEM((2, NZ, NY, *block), F32),
            buf(2, 4, NY, *block), buf(2, 4, NY, *block),
            buf(NZ, NY, *block), buf(NZ, NY, *block),
            buf(NZ, *block), buf(NZ, *block),
            buf(NY, *block), buf(NY, *block),
            pltpu.VMEM(block, F32), pltpu.VMEM(block, F32),
            pltpu.SemaphoreType.DMA((N_SEM,)), pltpu.SemaphoreType.DMA((N_SEM,)),
        ],
        compiler_params=pltpu.CompilerParams(
            collective_id=0, has_side_effects=True, vmem_limit_bytes=56 * 1024 * 1024,
        ),
    )(tokens, width_index.reshape(1, ROWS), up_weight, down_weight.T, cotangent)
    return mixed, gtok, gup, gdown.T


def solution(mesh):
    placed = (P("tok", "hid"), P("tok"), P("tok", "hid"), P("hid", "tok"), P("tok", "hid"))
    return jax.shard_map(
        per_device,
        mesh=mesh,
        in_specs=placed,
        out_specs=(P("tok", "hid"), P("tok", "hid"), P("tok", "hid"), P("hid", "tok")),
        check_vma=False,
    )
```

```python
import jax
import jax.numpy as jnp
from jax import lax
from jax.experimental import pallas as pl
from jax.experimental.pallas import tpu as pltpu
from jax.sharding import PartitionSpec as P

root_half = 0.7071067811865476
inv_root_tau = 0.3989422804014327
F32 = jnp.float32
BF16 = jnp.bfloat16
MESH = pl.DeviceIdType.MESH

ROWS = 512
COLS = 256
D = 1024
UNITS = 1024
NZ, NY = 8, 4
TILE = 256
N_SEM = 99
PHASES = dict(w=0, wc=1, x=2, o=3, g=4, r=5)

NT = (((1,), (1,)), ((), ()))
TN = (((0,), (0,)), ((), ()))


def gelu_pair(pre_act):
    cumul = 0.5 * (1.0 + lax.erf(pre_act * root_half))
    return (pre_act * cumul, cumul + pre_act * jnp.exp(-0.5 * pre_act * pre_act) * inv_root_tau)


def kernel(
    tok_ref, wid_ref, up_ref, down_ref, cot_ref,
    mixed_ref, gtok_ref, gup_ref, gdown_ref,
    uf, vf, xg, hbuf, pbuf, so, ro, fo, perm, permt,
    gsend, grecv, lane, rows_v, wid_v,
    sv, rv, su1, ru1, suz, ruz, svy, rvy, uy, vz,
    ssem, rsem, lsem,
):
    hid = lax.axis_index("hid")
    tok = lax.axis_index("tok")
    c = lax.rem(tok, 2)
    y = lax.rem(lax.div(tok, 2), NY)
    z = lax.div(tok, 2 * NY)

    def zmod(v):
        return lax.rem(v + 2 * NZ, NZ)

    def ymod(v):
        return lax.rem(v + 2 * NY, NY)

    def at(zz, yy, cc):
        return {"tok": (zz * NY + yy) * 2 + cc}

    zp, zm = at(zmod(z + 1), y, c), at(zmod(z - 1), y, c)
    mate = at(z, y, 1 - c)
    near = [at(zmod(z + k), y, c) for k in (1, -1, 2, -2, 3, -3, 4)]
    near += [at(z, ymod(y + r), c) for r in (1, 2, 3)] + [mate]
    xs = [{"hid": lax.rem(hid + k, 4)} for k in (1, 2, 3)]

    slots = {}
    sent = {}

    def slot(table, key):
        return table.setdefault(key, len(table))

    def send(key, src, dst, dev, size=1, phase="w", plane=None):
        sent[phase, plane] = sent.get((phase, plane), 0) + size
        pltpu.make_async_remote_copy(
            src_ref=src, dst_ref=dst, send_sem=ssem.at[PHASES[phase]],
            recv_sem=rsem.at[slot(slots, key)], device_id=dev, device_id_type=MESH,
        ).start()

    def recv(key, size=1):
        part = gsend.at[pl.ds(0, size)]
        pltpu.make_async_remote_copy(
            src_ref=part, dst_ref=part, send_sem=ssem.at[0],
            recv_sem=rsem.at[slot(slots, key)], device_id=mate, device_id_type=MESH,
        ).wait_recv()

    loads = [
        pltpu.make_async_copy(src, dst, lsem.at[i]) for i, (src, dst) in enumerate((
            (up_ref, uf.at[z, y, c]), (down_ref, vf.at[z, y, c]), (wid_ref, wid_v),
            (tok_ref, rows_v.at[0]), (cot_ref, rows_v.at[1]),
        ))
    ]
    for copy in loads:
        copy.start()

    barrier = pltpu.get_barrier_semaphore()
    for dev in near + xs:
        pl.semaphore_signal(barrier, inc=1, device_id=dev, device_id_type=MESH)

    loads[0].wait()
    loads[1].wait()
    pl.semaphore_wait(barrier, len(near) + len(xs))

    def peer_y(r):
        return ymod(y + r)

    def u_share(k):
        zz = zmod(z + k)
        for r in (1, 3, 2):
            ref = uf.at[zz, y, c]
            send(("uy", k), ref, ref, at(z, peer_y(r), c))

    def u_direct(k):
        ref = uf.at[z, y, c]
        send(("uz", k), ref, ref, at(zmod(z + k), y, c))

    def u_pass(k, step):
        ref = uf.at[zmod(z + k), y, c]
        send(("uz", step - k), ref, ref, at(zmod(z + step), y, c))

    def u_recv(k):
        recv(("uz", -k if k != 4 else 4))

    def u_group(k):
        recv(("uy", k), 3)
        zz = zmod(z + k)
        send("wc", uf.at[zz, :, c], uf.at[zz, :, c], mate, 4, "wc")

    def hops(r, d):
        return 4 if (r < 2) == (d == 0) else 3

    def v_send(r, d, s):
        zz = zmod(z - s) if d == 0 else zmod(z + s)
        ref = vf.at[zz, peer_y(r), c]
        send(("vz", r, d, s), ref, ref, zp if d == 0 else zm)

    def v_recv(r, d, s):
        if s < hops(r, d):
            recv(("vz", r, d, s))
            if s + 1 < hops(r, d):
                v_send(r, d, s + 1)

    def v_mate(k):
        zz = zmod(z + k)
        send("wc", vf.at[zz, :, c], vf.at[zz, :, c], mate, 4, "wc")

    own_v = vf.at[z, y, c]
    for r in (1, 3, 2):
        send(("vy", r), own_v, own_v, at(z, peer_y(r), c))
    v_send(0, 0, 0)
    v_send(0, 1, 0)
    u_direct(1)
    u_direct(-1)
    u_share(0)
    u_direct(2)
    u_direct(-2)
    u_direct(4)

    for copy in loads[2:]:
        copy.wait()
    wid = wid_v[...]
    level = lax.broadcasted_iota(jnp.int32, (8, ROWS), 0)
    ind = (jnp.broadcast_to(wid, (8, ROWS)) == level).astype(F32)
    ind16 = ind.astype(BF16)
    ia = lax.broadcasted_iota(jnp.int32, (ROWS, ROWS), 0)
    ib = lax.broadcasted_iota(jnp.int32, (ROWS, ROWS), 1)
    above = (ia < ib).astype(F32).astype(BF16)
    below = (ib < ia).astype(F32).astype(BF16)
    eye = (ia == ib).astype(F32).astype(BF16)
    counts = jnp.sum(ind, axis=1, keepdims=True)
    wider = [
        sum([counts[k:k + 1] for k in range(lo, 4)], jnp.zeros((1, 1), F32)) for lo in range(5)
    ]
    pre_row = jnp.dot(ind16, above, preferred_element_type=F32)
    pre_col = lax.dot_general(below, ind16, NT, preferred_element_type=F32)
    ind_col = lax.dot_general(eye, ind16, NT, preferred_element_type=F32)
    rank_row = sum([ind[k:k + 1] * (pre_row[k:k + 1] + wider[k + 1]) for k in range(4)])
    rank_col = sum(
        [ind_col[:, k:k + 1] * (pre_col[:, k:k + 1] + wider[k + 1]) for k in range(4)]
    )
    perm[...] = (ia == rank_row.astype(jnp.int32)).astype(F32).astype(BF16)
    permt[...] = (ib == rank_col.astype(jnp.int32)).astype(F32).astype(BF16)
    mine = pl.ds(pl.multiple_of(hid * COLS, COLS), COLS)
    for a in (0, 1):
        xg[a, :, mine] = jnp.dot(perm[...], rows_v[a], preferred_element_type=F32).astype(BF16)

    def xpart(h, lo, hi):
        return xg.at[:, pl.ds(lo, hi - lo), pl.ds(h * COLS, COLS)]

    def xsend(src, dst, h, lo, hi, key):
        part = xpart(h, lo, hi)
        send(key, part, part, xs[(dst - src) % 4 - 1], (hi - lo) // 32, "x", src)

    @pl.when(hid == 2)
    def _():
        xsend(2, 1, 2, 0, 128, "x0")
        xsend(2, 3, 2, 128, 256, "x0")
        xsend(2, 3, 2, 0, 64, "xm")
        xsend(2, 1, 2, 256, 384, "x1")
        xsend(2, 3, 2, 384, 512, "x1")

    @pl.when(hid == 1)
    def _():
        xsend(1, 0, 1, 0, 256, "x0")
        xsend(1, 2, 1, 0, 64, "xm")
        xsend(1, 3, 1, 0, 64, "xm")
        xsend(1, 0, 1, 256, 512, "x1")

    @pl.when(hid == 3)
    def _():
        xsend(3, 0, 3, 0, 256, "x0")
        xsend(3, 2, 3, 0, 64, "xm")
        xsend(3, 1, 3, 0, 128, "xm")
        xsend(3, 0, 3, 256, 512, "x1")

    @pl.when(hid == 0)
    def _():
        xsend(0, 1, 0, 0, 128, "xm")
        xsend(0, 3, 0, 0, 64, "xm")
        xsend(0, 2, 0, 0, 64, "xm")

    def forward_tokens(part):
        for plane, lo in ((1, 256 * part), (3, 256 * part + 128)):
            @pl.when(hid == plane)
            def _():
                recv(f"x{part}", 4)
                xsend(plane, 0, 2, lo, lo + 128, f"x{part}")

    for r in (3, 1, 2):
        recv(("vy", (4 - r) % 4))
        v_send(r, 0, 0)
        v_send(r, 1, 0)
    for k in (1, -1):
        u_recv(k)
        u_share(k)
    v_recv(0, 0, 0)
    v_recv(0, 1, 0)
    for k in (2, -2):
        u_recv(k)
        u_pass(k, -1 if k > 0 else 1)
        u_share(k)
    u_recv(4)
    u_share(4)
    forward_tokens(0)
    for r in (3, 1, 2):
        v_recv(r, 0, 0)
        v_recv(r, 1, 0)
    v_mate(0)
    v_mate(-1)
    v_mate(1)
    for k in (3, -3):
        u_recv(k)
        u_share(k)
    u_group(0)
    for r in range(4):
        v_recv(r, 0, 1)
        v_recv(r, 1, 1)
    v_mate(-2)
    v_mate(2)
    u_group(1)
    u_group(-1)
    forward_tokens(1)
    for r in range(4):
        v_recv(r, 0, 2)
        v_recv(r, 1, 2)
    v_mate(-3)
    v_mate(3)
    u_group(2)
    u_group(-2)
    u_group(4)
    for r in range(4):
        v_recv(r, 0, 3)
        v_recv(r, 1, 3)
    v_mate(4)
    u_group(3)
    u_group(-3)
    recv("wc", 64)

    def units(lo_row, n_row, lo_tile, hi_tile, count):
        rows = pl.ds(lo_row, n_row)

        def body(j, carry):
            cols = pl.ds(pl.multiple_of(j * TILE, TILE), TILE)
            u = uf[:, :, :, :, cols].reshape(D, TILE)
            v = vf[:, :, :, :, cols].reshape(D, TILE)
            pre = jnp.dot(xg[0, rows, :], u, preferred_element_type=F32)
            gh = jnp.dot(xg[1, rows, :], v, preferred_element_type=F32)
            act, slope = gelu_pair(pre)
            pg = gh * slope
            if count is not None:
                row = lax.broadcasted_iota(jnp.int32, (n_row, TILE), 0).astype(F32) + lo_row
                keep = row < count
                act = jnp.where(keep, act, 0.0)
                pg = jnp.where(keep, pg, 0.0)
            hbuf[rows, cols] = act.astype(BF16)
            pbuf[rows, cols] = pg.astype(BF16)
            return carry

        lax.fori_loop(lo_tile, hi_tile, body, 0)

    def outputs(plane, d, lo_row, n_row, n_unit):
        rows = pl.ds(lo_row, n_row)
        for a, val, w in ((0, hbuf, vf), (1, pbuf, uf)):
            wt = w[2 * d:2 * d + 2].reshape(COLS, UNITS)[:, :n_unit]
            out = lax.dot_general(val[rows, :n_unit], wt, NT, preferred_element_type=F32)
            if d == plane:
                ro[plane, a, rows, :] = out.astype(BF16)
            else:
                so[d, a, rows, :] = out.astype(BF16)

    def osend(src, dst, d, lo, hi, via=False):
        rows = pl.ds(lo, hi - lo)
        to = fo.at[:, rows, :] if via else ro.at[src, :, rows, :]
        send(f"f{lo // 256}" if via else "o", so.at[d, :, rows, :], to,
             xs[(dst - src) % 4 - 1], (hi - lo) // 32, "o", src)

    def tile(i):
        return lax.rem(lax.div(z, 2) + (2, 1, 3, 0)[i], 4)

    def grads(plane, n_row):
        for i in range(4):
            dt = tile(i)
            cols = pl.ds(pl.multiple_of(dt * COLS, COLS), COLS)
            zs = pl.ds(2 * dt, 2)
            for a, val in ((1, hbuf), (0, pbuf)):
                if plane == 0:
                    left = lax.dot_general(
                        xg[a, :, cols], val[:, :512], TN, preferred_element_type=F32)
                    right = lax.dot_general(
                        xg[a, :256, cols], val[:256, 512:], TN, preferred_element_type=F32)
                    g = jnp.concatenate([left, right], axis=1)
                else:
                    g = lax.dot_general(
                        xg[a, :n_row, cols], val[:n_row, :], TN, preferred_element_type=F32)
                g = g.reshape(2, NY, 2, 16, UNITS)
                lane[a, zs] = jnp.where(c == 0, g[:, :, 0], g[:, :, 1])
                part = pl.ds(32 * a + 8 * dt, 8)
                other = jnp.where(c == 0, g[:, :, 1], g[:, :, 0]).astype(BF16)
                gsend[part] = other.reshape(8, 16, UNITS)
                send(("gc", a, i), gsend.at[part], grecv.at[part], mate, 8, "g", plane)

    def mate_grads(a, tiles):
        for i in tiles:
            recv(("gc", a, i), 8)

    @pl.when(hid == 0)
    def _():
        recv("x0", 24)
        units(0, 256, 0, 2, None)
        units(0, 256, 2, 4, wider[1])
        for d in (2, 1, 3, 0):
            outputs(0, d, 0, 256, 1024)
            if d == 2:
                osend(0, 1, 2, 0, 128, True)
                osend(0, 3, 2, 128, 256, True)
            elif d:
                osend(0, d, d, 0, 256)
        recv("x1", 24)
        units(256, 256, 0, 2, None)
        grads(0, 512)
        for d in (2, 1, 3, 0):
            outputs(0, d, 256, 256, 512)
            if d == 2:
                osend(0, 1, 2, 256, 384, True)
                osend(0, 3, 2, 384, 512, True)
            elif d:
                osend(0, d, d, 256, 512)

    for plane, n_row, n_in, dests in (
        (1, 128, 8, (0, 3, 2, 1)), (2, 64, 6, (0, 1, 3, 2)), (3, 64, 6, (1, 0, 2, 3)),
    ):
        @pl.when(hid == plane)
        def _():
            recv("xm", n_in)
            units(0, n_row, 0, 4, wider[min(plane + 1, 3)])
            for d in dests:
                outputs(plane, d, 0, n_row, 1024)
                if d != plane:
                    osend(plane, d, d, 0, n_row)
            grads(plane, n_row)

    def forward_outputs(part):
        for plane, lo in ((1, 256 * part), (3, 256 * part + 128)):
            @pl.when(hid == plane)
            def _():
                recv(f"f{part}", 4)
                rows = pl.ds(lo, 128)
                send("o", fo.at[:, rows, :], ro.at[0, :, rows, :], xs[(2 - plane) % 4 - 1], 4,
                     "o", plane)

    def total(a, zz, yy):
        return lane[a, zz, yy] + grecv[32 * a + 4 * zz + yy].astype(F32)

    def ring_send(r, d, s):
        zz = zmod(z + 4 - s) if d == 0 else zmod(z - 4 + s)
        val = total(1, zz, peer_y(r))
        if s > 4 - hops(r, d):
            val = val + rv[d, s - 1, r].astype(F32)
        sv[d, s, r] = val.astype(BF16)
        send(("v", r, d, s), sv.at[d, s, r], rv.at[d, s, r], zp if d == 0 else zm, 1, "r")

    def ring_step(s):
        for r in range(4):
            for d in (0, 1):
                if s > 4 - hops(r, d):
                    recv(("v", r, d, s - 1))
                if s >= 4 - hops(r, d):
                    ring_send(r, d, s)

    def up_share(k):
        for r in (1, 3, 2):
            su1[k + 3, r] = total(0, zmod(z + k), peer_y(r)).astype(BF16)
            send(("uu", k), su1.at[k + 3, r], ru1.at[k + 3, r], at(z, peer_y(r), c), 1, "r")

    def up_sum(k):
        val = total(0, zmod(z + k), y)
        recv(("uu", k), 3)
        for r in (1, 3, 2):
            val = val + ru1[k + 3, r].astype(F32)
        return val

    def up_direct(k):
        suz[k + 3] = up_sum(k).astype(BF16)
        send("uw", suz.at[k + 3], ruz.at[k + 3], at(zmod(z + k), y, c), 1, "r")

    mate_grads(1, (0,))
    ring_step(0)
    mate_grads(0, (0,))
    up_share(4)
    mate_grads(1, (1, 2))
    ring_step(1)
    mate_grads(0, (1, 2))
    for k in (3, -3, 2, -2):
        up_share(k)
    forward_outputs(0)
    mate_grads(1, (3,))
    ring_step(2)
    mate_grads(0, (3,))
    for k in (1, -1, 0):
        up_share(k)
    up_direct(4)
    up_direct(3)
    up_direct(-3)
    ring_step(3)
    forward_outputs(1)
    up_direct(2)
    up_direct(-2)
    up_direct(1)
    up_direct(-1)
    uy[...] = up_sum(0)
    for r in (1, 3, 2, 0):
        val = total(1, z, peer_y(r))
        for d in (0, 1):
            recv(("v", r, d, 3))
            val = val + rv[d, 3, r].astype(F32)
        if r:
            svy[r] = val.astype(BF16)
            send("vw", svy.at[r], rvy.at[r], at(z, peer_y(r), c), 1, "r")
        else:
            vz[...] = val

    for plane, n_in in ((0, 8), (1, 20), (2, 22), (3, 22)):
        @pl.when(hid == plane)
        def _():
            recv("o", n_in)

    for a, ref in ((0, mixed_ref), (1, gtok_ref)):
        top = ro[0, a, 0:128].astype(F32) + ro[1, a, 0:128].astype(F32)
        wide = top[:64] + ro[2, a, 0:64].astype(F32) + ro[3, a, 0:64].astype(F32)
        ro[0, a, 0:128] = jnp.concatenate([wide, top[64:]], axis=0).astype(BF16)
        ref[...] = jnp.dot(permt[...], ro[0, a], preferred_element_type=F32).astype(BF16)

    val = vz[...]
    recv("vw", 3)
    for r in (1, 3, 2):
        val = val + rvy[r].astype(F32)
    gdown_ref[...] = val
    val = uy[...]
    recv("uw", 7)
    for k in (4, 3, -3, 2, -2, 1, -1):
        val = val + ruz[k + 3].astype(F32)
    gup_ref[...] = val

    def left(phase, plane):
        part = gsend.at[pl.ds(0, sent[phase, plane])]
        pltpu.make_async_remote_copy(
            src_ref=part, dst_ref=part, send_sem=ssem.at[PHASES[phase]], recv_sem=rsem.at[0],
            device_id=mate, device_id_type=MESH,
        ).wait_send()

    for phase in ("w", "wc", "r"):
        left(phase, None)
    for plane in range(4):
        @pl.when(hid == plane)
        def _():
            for phase in ("x", "o", "g"):
                left(phase, plane)
    assert len(slots) == N_SEM, len(slots)


def store(*refs):
    sem = refs[-1]
    copies = [pltpu.make_async_copy(refs[i], refs[4 + i], sem.at[i]) for i in range(4)]
    for copy in copies:
        copy.start()
    for copy in copies:
        copy.wait()


def per_device(tokens, width_index, up_weight, down_weight, cotangent):
    vm = pl.BlockSpec(memory_space=pltpu.VMEM)
    hbm = pl.BlockSpec(memory_space=pltpu.HBM)
    block = (16, UNITS)
    shapes = [((ROWS, COLS), BF16), ((ROWS, COLS), BF16), (block, F32), (block, F32)]

    def buf(*shape):
        return pltpu.VMEM(shape, BF16)

    results = pl.pallas_call(
        kernel,
        out_shape=tuple(pltpu.VMEM(*shape) for shape in shapes),
        in_specs=[hbm] * 5,
        out_specs=(vm,) * 4,
        scratch_shapes=[
            buf(NZ, NY, 2, *block), buf(NZ, NY, 2, *block),
            buf(2, ROWS, D), buf(ROWS, UNITS), buf(ROWS, UNITS),
            buf(4, 2, ROWS, COLS), buf(4, 2, ROWS, COLS), buf(2, ROWS, COLS),
            buf(ROWS, ROWS), buf(ROWS, ROWS),
            buf(64, *block), buf(64, *block),
            pltpu.VMEM((2, NZ, NY, *block), F32),
            buf(2, ROWS, COLS), pltpu.VMEM((1, ROWS), jnp.int32),
            buf(2, 4, NY, *block), buf(2, 4, NY, *block),
            buf(NZ, NY, *block), buf(NZ, NY, *block),
            buf(NZ, *block), buf(NZ, *block),
            buf(NY, *block), buf(NY, *block),
            pltpu.VMEM(block, F32), pltpu.VMEM(block, F32),
            pltpu.SemaphoreType.DMA((len(PHASES),)), pltpu.SemaphoreType.DMA((N_SEM,)),
            pltpu.SemaphoreType.DMA((5,)),
        ],
        compiler_params=pltpu.CompilerParams(
            collective_id=0, has_side_effects=True, vmem_limit_bytes=48 * 1024 * 1024,
        ),
    )(*[
        pltpu.with_memory_space_constraint(x, pltpu.HBM)
        for x in (tokens, width_index.reshape(1, ROWS), up_weight, down_weight.T, cotangent)
    ])
    mixed, gtok, gup, gdown = pl.pallas_call(
        store,
        out_shape=tuple(jax.ShapeDtypeStruct(*shape) for shape in shapes),
        in_specs=[vm] * 4,
        out_specs=(hbm,) * 4,
        scratch_shapes=[pltpu.SemaphoreType.DMA((4,))],
    )(*[pltpu.with_memory_space_constraint(x, pltpu.VMEM) for x in results])
    return mixed, gtok, gup, gdown.T


def solution(mesh):
    placed = (P("tok", "hid"), P("tok"), P("tok", "hid"), P("hid", "tok"), P("tok", "hid"))
    return jax.shard_map(
        per_device,
        mesh=mesh,
        in_specs=placed,
        out_specs=(P("tok", "hid"), P("tok", "hid"), P("tok", "hid"), P("hid", "tok")),
        check_vma=False,
    )
```

```python
import jax
import jax.numpy as jnp
from jax import lax
from jax.experimental import pallas as pl
from jax.experimental.pallas import tpu as pltpu
from jax.sharding import PartitionSpec as P

root_half = 0.7071067811865476
inv_root_tau = 0.3989422804014327
F32 = jnp.float32
BF16 = jnp.bfloat16
MESH = pl.DeviceIdType.MESH

ROWS = 512
COLS = 256
D = 1024
UNITS = 1024
NZ, NY = 8, 4
TILE = 256
HALF = 512
N_SEM = 119
GROUP = (0, 1, 1, 2)
PHASES = dict(w=0, wc=1, x=2, o=3, g=4, r=5)

NT = (((1,), (1,)), ((), ()))
TN = (((0,), (0,)), ((), ()))


def gelu_pair(pre_act):
    cumul = 0.5 * (1.0 + lax.erf(pre_act * root_half))
    return (pre_act * cumul, cumul + pre_act * jnp.exp(-0.5 * pre_act * pre_act) * inv_root_tau)


def kernel(
    tok_ref, wid_ref, up_ref, down_ref, cot_ref,
    mixed_ref, gtok_ref, gup_ref, gdown_ref,
    uf, vf, xg, hbuf, pbuf, so, ro, fo, perm, permt,
    gsend, grecv, lane, rows_v, wid_v,
    sv, rv, su1, ru1, suz, ruz, svy, rvy, uy, vz,
    ssem, rsem, lsem,
):
    hid = lax.axis_index("hid")
    tok = lax.axis_index("tok")
    c = lax.rem(tok, 2)
    y = lax.rem(lax.div(tok, 2), NY)
    z = lax.div(tok, 2 * NY)

    def zmod(v):
        return lax.rem(v + 2 * NZ, NZ)

    def ymod(v):
        return lax.rem(v + 2 * NY, NY)

    def halves(h):
        return pl.ds(HALF * h, HALF)

    def at(zz, yy, cc):
        return {"tok": (zz * NY + yy) * 2 + cc}

    zp, zm = at(zmod(z + 1), y, c), at(zmod(z - 1), y, c)
    mate = at(z, y, 1 - c)
    near = [at(zmod(z + k), y, c) for k in (1, -1, 2, -2)]
    near += [at(z, ymod(y + r), c) for r in (1, 2, 3)] + [mate]
    xs = [{"hid": lax.rem(hid + k, 4)} for k in (1, 2, 3)]

    def stand_in(size):
        if size == int(size):
            return gsend.at[pl.ds(0, int(size))]
        return gsend.at[pl.ds(0, int(2 * size)), :, pl.ds(0, HALF)]

    slots = {}
    sent = {}

    def slot(table, key):
        return table.setdefault(key, len(table))

    def send(key, src, dst, dev, size=1, phase="w", plane=None):
        sent[phase, plane] = sent.get((phase, plane), 0) + size
        pltpu.make_async_remote_copy(
            src_ref=src, dst_ref=dst, send_sem=ssem.at[PHASES[phase]],
            recv_sem=rsem.at[slot(slots, key)], device_id=dev, device_id_type=MESH,
        ).start()

    def recv(key, size=1):
        part = stand_in(size)
        pltpu.make_async_remote_copy(
            src_ref=part, dst_ref=part, send_sem=ssem.at[0],
            recv_sem=rsem.at[slot(slots, key)], device_id=mate, device_id_type=MESH,
        ).wait_recv()

    loads = [
        pltpu.make_async_copy(src, dst, lsem.at[i]) for i, (src, dst) in enumerate((
            (up_ref, uf.at[z, y, c]), (down_ref, vf.at[z, y, c]), (wid_ref, wid_v),
            (tok_ref, rows_v.at[0]), (cot_ref, rows_v.at[1]),
        ))
    ]
    for copy in loads:
        copy.start()

    barrier = pltpu.get_barrier_semaphore()
    for dev in near + xs:
        pl.semaphore_signal(barrier, inc=1, device_id=dev, device_id_type=MESH)

    loads[0].wait()
    loads[1].wait()
    pl.semaphore_wait(barrier, len(near) + len(xs))

    def peer_y(r):
        return ymod(y + r)

    def u_share(k):
        zz = zmod(z + k)
        for r in (1, 3, 2):
            ref = uf.at[zz, y, c]
            send(("uy", k), ref, ref, at(z, peer_y(r), c))

    def u_direct(k):
        ref = uf.at[z, y, c]
        send(("uz", k), ref, ref, at(zmod(z + k), y, c))

    def u_pass(k):
        near, far, cols = (-1, -2, halves(1)) if k > 0 else (1, 2, halves(0))
        ref = uf.at[zmod(z + k), y, c]
        send(("uz", near - k), ref, ref, at(zmod(z + near), y, c))
        ref = uf.at[zmod(z + k), y, c, :, cols]
        send(("uz", 4), ref, ref, at(zmod(z + far), y, c), 0.5)

    def u_recv(k):
        recv(("uz", -k if k != 4 else 4))

    def u_group(k):
        recv(("uy", k), 3)
        zz = zmod(z + k)
        send("wc", uf.at[zz, :, c], uf.at[zz, :, c], mate, 4, "wc")

    def hops(r, d):
        return 4 if (r < 2) == (d == 0) else 3

    def v_send(r, d, s):
        zz = zmod(z - s) if d == 0 else zmod(z + s)
        ref = vf.at[zz, peer_y(r), c]
        send(("vz", r, d, s), ref, ref, zp if d == 0 else zm)

    def v_mate(r, zz):
        ref = vf.at[zz, peer_y(r), c]
        send("wc", ref, ref, mate, 1, "wc")

    def v_recv(r, d, s):
        if s < hops(r, d):
            recv(("vz", r, d, s))
            if s + 1 < hops(r, d):
                v_send(r, d, s + 1)
            v_mate(r, zmod(z - s - 1) if d == 0 else zmod(z + s + 1))

    own_v = vf.at[z, y, c]
    for r in (1, 3, 2):
        send(("vy", r), own_v, own_v, at(z, peer_y(r), c))
    v_send(0, 0, 0)
    v_send(0, 1, 0)
    u_direct(1)
    u_direct(-1)
    u_share(0)
    u_direct(2)
    u_direct(-2)

    for copy in loads[2:]:
        copy.wait()
    wid = wid_v[...]
    level = lax.broadcasted_iota(jnp.int32, (8, ROWS), 0)
    ind = (jnp.broadcast_to(wid, (8, ROWS)) == level).astype(F32)
    ind16 = ind.astype(BF16)
    ia = lax.broadcasted_iota(jnp.int32, (ROWS, ROWS), 0)
    ib = lax.broadcasted_iota(jnp.int32, (ROWS, ROWS), 1)
    above = (ia < ib).astype(F32).astype(BF16)
    below = (ib < ia).astype(F32).astype(BF16)
    eye = (ia == ib).astype(F32).astype(BF16)
    counts = jnp.sum(ind, axis=1, keepdims=True)
    wider = [
        sum([counts[k:k + 1] for k in range(lo, 4)], jnp.zeros((1, 1), F32)) for lo in range(5)
    ]
    pre_row = jnp.dot(ind16, above, preferred_element_type=F32)
    pre_col = lax.dot_general(below, ind16, NT, preferred_element_type=F32)
    ind_col = lax.dot_general(eye, ind16, NT, preferred_element_type=F32)
    rank_row = sum([ind[k:k + 1] * (pre_row[k:k + 1] + wider[k + 1]) for k in range(4)])
    rank_col = sum(
        [ind_col[:, k:k + 1] * (pre_col[:, k:k + 1] + wider[k + 1]) for k in range(4)]
    )
    perm[...] = (ia == rank_row.astype(jnp.int32)).astype(F32).astype(BF16)
    permt[...] = (ib == rank_col.astype(jnp.int32)).astype(F32).astype(BF16)
    mine = pl.ds(pl.multiple_of(hid * COLS, COLS), COLS)
    for a in (0, 1):
        xg[a, :, mine] = jnp.dot(perm[...], rows_v[a], preferred_element_type=F32).astype(BF16)

    def xpart(h, lo, hi):
        return xg.at[:, pl.ds(lo, hi - lo), pl.ds(h * COLS, COLS)]

    def xsend(src, dst, h, lo, hi, key):
        part = xpart(h, lo, hi)
        send(key, part, part, xs[(dst - src) % 4 - 1], (hi - lo) // 32, "x", src)

    @pl.when(hid == 2)
    def _():
        xsend(2, 1, 2, 0, 128, "x0")
        xsend(2, 3, 2, 128, 256, "x0")
        xsend(2, 3, 2, 0, 64, "xm")
        xsend(2, 1, 2, 256, 384, "x1")
        xsend(2, 3, 2, 384, 512, "x1")

    @pl.when(hid == 1)
    def _():
        xsend(1, 0, 1, 0, 256, "x0")
        xsend(1, 2, 1, 0, 64, "xm")
        xsend(1, 3, 1, 0, 64, "xm")
        xsend(1, 0, 1, 256, 512, "x1")

    @pl.when(hid == 3)
    def _():
        xsend(3, 0, 3, 0, 256, "x0")
        xsend(3, 2, 3, 0, 64, "xm")
        xsend(3, 1, 3, 0, 128, "xm")
        xsend(3, 0, 3, 256, 512, "x1")

    @pl.when(hid == 0)
    def _():
        xsend(0, 1, 0, 0, 128, "xm")
        xsend(0, 3, 0, 0, 64, "xm")
        xsend(0, 2, 0, 0, 64, "xm")

    def forward_tokens(part):
        for plane, lo in ((1, 256 * part), (3, 256 * part + 128)):
            @pl.when(hid == plane)
            def _():
                recv(f"x{part}", 4)
                xsend(plane, 0, 2, lo, lo + 128, f"x{part}")

    for r in (3, 1, 2):
        recv(("vy", (4 - r) % 4))
        v_send(r, 0, 0)
        v_send(r, 1, 0)
        v_mate(r, z)
    v_mate(0, z)
    for k in (1, -1):
        u_recv(k)
        u_share(k)
    v_recv(0, 0, 0)
    v_recv(0, 1, 0)
    for k in (2, -2):
        u_recv(k)
        u_pass(k)
        u_share(k)
    forward_tokens(0)
    for r in (3, 1, 2):
        v_recv(r, 0, 0)
        v_recv(r, 1, 0)
    for k in (3, -3, 4):
        u_recv(k)
        u_share(k)
    u_group(0)
    for r in range(4):
        v_recv(r, 0, 1)
        v_recv(r, 1, 1)
    u_group(1)
    u_group(-1)
    forward_tokens(1)
    for r in range(4):
        v_recv(r, 0, 2)
        v_recv(r, 1, 2)
    u_group(2)
    u_group(-2)
    for r in range(4):
        v_recv(r, 0, 3)
        v_recv(r, 1, 3)
    u_group(3)
    u_group(-3)
    u_group(4)
    recv("wc", 64)

    def units(lo_row, n_row, lo_tile, hi_tile, count):
        rows = pl.ds(lo_row, n_row)

        def body(j, carry):
            cols = pl.ds(pl.multiple_of(j * TILE, TILE), TILE)
            u = uf[:, :, :, :, cols].reshape(D, TILE)
            v = vf[:, :, :, :, cols].reshape(D, TILE)
            pre = jnp.dot(xg[0, rows, :], u, preferred_element_type=F32)
            gh = jnp.dot(xg[1, rows, :], v, preferred_element_type=F32)
            act, slope = gelu_pair(pre)
            pg = gh * slope
            if count is not None:
                row = lax.broadcasted_iota(jnp.int32, (n_row, TILE), 0).astype(F32) + lo_row
                keep = row < count
                act = jnp.where(keep, act, 0.0)
                pg = jnp.where(keep, pg, 0.0)
            hbuf[rows, cols] = act.astype(BF16)
            pbuf[rows, cols] = pg.astype(BF16)
            return carry

        lax.fori_loop(lo_tile, hi_tile, body, 0)

    def outputs(plane, d, lo_row, n_row, n_unit):
        rows = pl.ds(lo_row, n_row)
        for a, val, w in ((0, hbuf, vf), (1, pbuf, uf)):
            wt = w[2 * d:2 * d + 2].reshape(COLS, UNITS)[:, :n_unit]
            out = lax.dot_general(val[rows, :n_unit], wt, NT, preferred_element_type=F32)
            if d == plane:
                ro[plane, a, rows, :] = out.astype(BF16)
            else:
                so[d, a, rows, :] = out.astype(BF16)

    def osend(src, dst, d, lo, hi, via=False):
        rows = pl.ds(lo, hi - lo)
        to = fo.at[:, rows, :] if via else ro.at[src, :, rows, :]
        send(f"f{lo // 256}" if via else "o", so.at[d, :, rows, :], to,
             xs[(dst - src) % 4 - 1], (hi - lo) // 32, "o", src)

    def tile(i):
        return lax.rem(lax.div(z, 2) + (2, 1, 3, 0)[i], 4)

    def grads(plane, n_row, h):
        hc = halves(h)
        for i in range(4):
            dt = tile(i)
            cols = pl.ds(pl.multiple_of(dt * COLS, COLS), COLS)
            zs = pl.ds(2 * dt, 2)
            for a, val in ((1, hbuf), (0, pbuf)):
                g = lax.dot_general(
                    xg[a, :n_row, cols], val[:n_row, hc], TN, preferred_element_type=F32)
                g = g.reshape(2, NY, 2, 16, HALF)
                lane[a, zs, :, :, hc] = jnp.where(c == 0, g[:, :, 0], g[:, :, 1])
                part = pl.ds(32 * a + 8 * dt, 8)
                other = jnp.where(c == 0, g[:, :, 1], g[:, :, 0]).astype(BF16)
                gsend[part, :, hc] = other.reshape(8, 16, HALF)
                send(("gc", h, a, GROUP[i]), gsend.at[part, :, hc], grecv.at[part, :, hc], mate,
                     4, "g", plane)

    def mate_grads(h, a, group):
        recv(("gc", h, a, group), 8 if group == 1 else 4)

    others = (
        (1, 128, 8, (0, 3, 2, 1)), (2, 64, 6, (0, 1, 3, 2)), (3, 64, 6, (1, 0, 2, 3)),
    )

    def row_outputs(lo, n_unit):
        for d in (2, 1, 3, 0):
            outputs(0, d, lo, 256, n_unit)
            if d == 2:
                osend(0, 1, 2, lo, lo + 128, True)
                osend(0, 3, 2, lo + 128, lo + 256, True)
            elif d:
                osend(0, d, d, lo, lo + 256)

    @pl.when(hid == 0)
    def _():
        recv("x0", 24)
        units(0, 256, 2, 4, wider[1])
        grads(0, 256, 1)
        units(0, 256, 0, 2, None)

    for plane, n_row, n_in, dests in others:
        @pl.when(hid == plane)
        def _():
            recv("xm", n_in)
            count = wider[min(plane + 1, 3)]
            units(0, n_row, 2, 4, count)
            grads(plane, n_row, 1)
            units(0, n_row, 0, 2, count)
            for d in dests:
                outputs(plane, d, 0, n_row, UNITS)
                if d != plane:
                    osend(plane, d, d, 0, n_row)

    def rest_of_rows():
        @pl.when(hid == 0)
        def _():
            recv("x1", 24)
            units(256, 256, 0, 2, None)
            grads(0, 512, 0)
            row_outputs(0, UNITS)

        for plane, n_row, _, _ in others:
            @pl.when(hid == plane)
            def _():
                grads(plane, n_row, 0)

    def forward_outputs(part):
        for plane, lo in ((1, 256 * part), (3, 256 * part + 128)):
            @pl.when(hid == plane)
            def _():
                recv(f"f{part}", 4)
                rows = pl.ds(lo, 128)
                send("o", fo.at[:, rows, :], ro.at[0, :, rows, :], xs[(2 - plane) % 4 - 1], 4,
                     "o", plane)

    def total(h, a, zz, yy):
        hc = halves(h)
        return lane[a, zz, yy, :, hc] + grecv[32 * a + 4 * zz + yy, :, hc].astype(F32)

    def steps(p, d):
        return 4 if p == d else 3

    def ring(h, s):
        hc = halves(h)
        for p in (0, 1):
            for d in (0, 1):
                first = 4 - steps(p, d)
                ys = pl.ds(2 * p, 2)
                if s > first:
                    recv(("v", h, p, d, s - 1))
                if s < first:
                    continue
                zz = zmod(z + 4 - s) if d == 0 else zmod(z - 4 + s)
                for r in (2 * p, 2 * p + 1):
                    val = total(h, 1, zz, peer_y(r))
                    if s > first:
                        val = val + rv[d, s - 1, r, :, hc].astype(F32)
                    sv[d, s, r, :, hc] = val.astype(BF16)
                send(("v", h, p, d, s), sv.at[d, s, ys, :, hc], rv.at[d, s, ys, :, hc],
                     zp if d == 0 else zm, 1, "r")

    def ring_end(h):
        hc = halves(h)
        for p in (1, 0):
            for d in (0, 1):
                recv(("v", h, p, d, 3))
            for r in (2 * p + 1, 2 * p):
                val = total(h, 1, z, peer_y(r))
                for d in (0, 1):
                    val = val + rv[d, 3, r, :, hc].astype(F32)
                if r:
                    svy[r, :, hc] = val.astype(BF16)
                    send(("vw", h), svy.at[r, :, hc], rvy.at[r, :, hc], at(z, peer_y(r), c),
                         0.5, "r")
                else:
                    vz[:, hc] = val

    def up_share(h, k):
        hc = halves(h)
        for r in (1, 3, 2):
            su1[k + 3, r, :, hc] = total(h, 0, zmod(z + k), peer_y(r)).astype(BF16)
            send(("uu", h, k), su1.at[k + 3, r, :, hc], ru1.at[k + 3, r, :, hc],
                 at(z, peer_y(r), c), 0.5, "r")

    def up_sum(h, k):
        hc = halves(h)
        val = total(h, 0, zmod(z + k), y)
        recv(("uu", h, k), 1.5)
        for r in (1, 3, 2):
            val = val + ru1[k + 3, r, :, hc].astype(F32)
        return val

    def up_send(h, k, val, key, hop):
        hc = halves(h)
        suz[k + 3, :, hc] = val.astype(BF16)
        send(key, suz.at[k + 3, :, hc], ruz.at[k + 3, :, hc], at(zmod(z + hop), y, c), 0.5, "r")

    def up_far(h):
        up_send(h, 4, up_sum(h, 4), ("uf", h, 4), 2 if h == 0 else -2)
        up_send(h, 3, up_sum(h, 3), ("uf", h, 3), 1)
        up_send(h, -3, up_sum(h, -3), ("uf", h, -3), -1)

    def up_near(h):
        for k in (1, -1):
            up_send(h, k, up_sum(h, k), ("ue", h), k)

    def up_two(h):
        hc = halves(h)
        for k, far in ((2, 3), (-2, -3)):
            val = up_sum(h, k)
            recv(("uf", h, far), 0.5)
            val = val + ruz[far + 3, :, hc].astype(F32)
            if (k == 2) == (h == 0):
                recv(("uf", h, 4), 0.5)
                val = val + ruz[7, :, hc].astype(F32)
            up_send(h, k, val, ("ue", h), k)

    def start_half(h):
        mate_grads(h, 1, 0)
        ring(h, 0)
        mate_grads(h, 0, 0)
        up_share(h, 4)
        mate_grads(h, 0, 1)
        for k in (3, -3, 2, -2):
            up_share(h, k)
        mate_grads(h, 0, 2)
        for k in (1, -1, 0):
            up_share(h, k)
        mate_grads(h, 1, 1)
        mate_grads(h, 1, 2)

    start_half(1)
    rest_of_rows()
    start_half(0)
    ring(1, 1)
    up_far(1)

    @pl.when(hid == 0)
    def _():
        row_outputs(256, HALF)

    ring(0, 1)
    ring(1, 2)
    up_near(1)
    up_far(0)
    forward_outputs(0)
    ring(0, 2)
    ring(1, 3)
    up_two(1)
    up_near(0)
    ring(0, 3)
    ring_end(1)
    uy[:, halves(1)] = up_sum(1, 0)
    up_two(0)
    forward_outputs(1)
    uy[:, halves(0)] = up_sum(0, 0)
    ring_end(0)

    for plane, n_in in ((0, 8), (1, 20), (2, 22), (3, 22)):
        @pl.when(hid == plane)
        def _():
            recv("o", n_in)

    for a, ref in ((0, mixed_ref), (1, gtok_ref)):
        top = ro[0, a, 0:128].astype(F32) + ro[1, a, 0:128].astype(F32)
        wide = top[:64] + ro[2, a, 0:64].astype(F32) + ro[3, a, 0:64].astype(F32)
        ro[0, a, 0:128] = jnp.concatenate([wide, top[64:]], axis=0).astype(BF16)
        ref[...] = jnp.dot(permt[...], ro[0, a], preferred_element_type=F32).astype(BF16)

    for h in (1, 0):
        hc = halves(h)
        recv(("vw", h), 1.5)
        val = vz[:, hc]
        for r in (1, 3, 2):
            val = val + rvy[r, :, hc].astype(F32)
        gdown_ref[:, hc] = val
        recv(("ue", h), 2)
        val = uy[:, hc]
        for k in (1, -1, 2, -2):
            val = val + ruz[k + 3, :, hc].astype(F32)
        gup_ref[:, hc] = val

    def left(phase, plane):
        part = stand_in(sent[phase, plane])
        pltpu.make_async_remote_copy(
            src_ref=part, dst_ref=part, send_sem=ssem.at[PHASES[phase]], recv_sem=rsem.at[0],
            device_id=mate, device_id_type=MESH,
        ).wait_send()

    for phase in ("w", "wc", "r"):
        left(phase, None)
    for plane in range(4):
        @pl.when(hid == plane)
        def _():
            for phase in ("x", "o", "g"):
                left(phase, plane)
    assert len(slots) == N_SEM, len(slots)


def store(*refs):
    sem = refs[-1]
    copies = [pltpu.make_async_copy(refs[i], refs[4 + i], sem.at[i]) for i in range(4)]
    for copy in copies:
        copy.start()
    for copy in copies:
        copy.wait()


def per_device(tokens, width_index, up_weight, down_weight, cotangent):
    vm = pl.BlockSpec(memory_space=pltpu.VMEM)
    hbm = pl.BlockSpec(memory_space=pltpu.HBM)
    block = (16, UNITS)
    shapes = [((ROWS, COLS), BF16), ((ROWS, COLS), BF16), (block, F32), (block, F32)]

    def buf(*shape):
        return pltpu.VMEM(shape, BF16)

    results = pl.pallas_call(
        kernel,
        out_shape=tuple(pltpu.VMEM(*shape) for shape in shapes),
        in_specs=[hbm] * 5,
        out_specs=(vm,) * 4,
        scratch_shapes=[
            buf(NZ, NY, 2, *block), buf(NZ, NY, 2, *block),
            buf(2, ROWS, D), buf(ROWS, UNITS), buf(ROWS, UNITS),
            buf(4, 2, ROWS, COLS), buf(4, 2, ROWS, COLS), buf(2, ROWS, COLS),
            buf(ROWS, ROWS), buf(ROWS, ROWS),
            buf(64, *block), buf(64, *block),
            pltpu.VMEM((2, NZ, NY, *block), F32),
            buf(2, ROWS, COLS), pltpu.VMEM((1, ROWS), jnp.int32),
            buf(2, 4, NY, *block), buf(2, 4, NY, *block),
            buf(NZ, NY, *block), buf(NZ, NY, *block),
            buf(NZ, *block), buf(NZ, *block),
            buf(NY, *block), buf(NY, *block),
            pltpu.VMEM(block, F32), pltpu.VMEM(block, F32),
            pltpu.SemaphoreType.DMA((len(PHASES),)), pltpu.SemaphoreType.DMA((N_SEM,)),
            pltpu.SemaphoreType.DMA((5,)),
        ],
        compiler_params=pltpu.CompilerParams(
            collective_id=0, has_side_effects=True, vmem_limit_bytes=48 * 1024 * 1024,
        ),
    )(*[
        pltpu.with_memory_space_constraint(x, pltpu.HBM)
        for x in (tokens, width_index.reshape(1, ROWS), up_weight, down_weight.T, cotangent)
    ])
    mixed, gtok, gup, gdown = pl.pallas_call(
        store,
        out_shape=tuple(jax.ShapeDtypeStruct(*shape) for shape in shapes),
        in_specs=[vm] * 4,
        out_specs=(hbm,) * 4,
        scratch_shapes=[pltpu.SemaphoreType.DMA((4,))],
    )(*[pltpu.with_memory_space_constraint(x, pltpu.VMEM) for x in results])
    return mixed, gtok, gup, gdown.T


def solution(mesh):
    placed = (P("tok", "hid"), P("tok"), P("tok", "hid"), P("hid", "tok"), P("tok", "hid"))
    return jax.shard_map(
        per_device,
        mesh=mesh,
        in_specs=placed,
        out_specs=(P("tok", "hid"), P("tok", "hid"), P("tok", "hid"), P("hid", "tok")),
        check_vma=False,
    )
```

```python
import jax
import jax.numpy as jnp
from jax import lax
from jax.experimental import pallas as pl
from jax.experimental.pallas import tpu as pltpu
from jax.sharding import PartitionSpec as P

root_half = 0.7071067811865476
inv_root_tau = 0.3989422804014327
F32 = jnp.float32
BF16 = jnp.bfloat16
MESH = pl.DeviceIdType.MESH

ROWS = 512
COLS = 256
D = 1024
UNITS = 1024
NZ, NY = 8, 4
TILE = 256
HALF = 512
N_SEM = 119
GROUP = (0, 1, 1, 2)
PHASES = dict(w=0, wc=1, x=2, o=3, g=4, r=5)

NT = (((1,), (1,)), ((), ()))
TN = (((0,), (0,)), ((), ()))


def gelu_pair(pre_act):
    cumul = 0.5 * (1.0 + lax.erf(pre_act * root_half))
    return (pre_act * cumul, cumul + pre_act * jnp.exp(-0.5 * pre_act * pre_act) * inv_root_tau)


def kernel(
    tok_ref, wid_ref, up_ref, down_ref, cot_ref,
    mixed_ref, gtok_ref, gup_ref, gdown_ref,
    uf, vf, xg, hbuf, pbuf, so, ro, fo, perm, permt,
    gsend, grecv, lane, rows_v, wid_v,
    sv, rv, su1, ru1, suz, ruz, svy, rvy, uy, vz,
    ssem, rsem, lsem,
):
    hid = lax.axis_index("hid")
    tok = lax.axis_index("tok")
    c = lax.rem(tok, 2)
    y = lax.rem(lax.div(tok, 2), NY)
    z = lax.div(tok, 2 * NY)

    def zmod(v):
        return lax.rem(v + 2 * NZ, NZ)

    def ymod(v):
        return lax.rem(v + 2 * NY, NY)

    def halves(h):
        return pl.ds(HALF * h, HALF)

    def at(zz, yy, cc):
        return {"tok": (zz * NY + yy) * 2 + cc}

    zp, zm = at(zmod(z + 1), y, c), at(zmod(z - 1), y, c)
    mate = at(z, y, 1 - c)
    near = [at(zmod(z + k), y, c) for k in (1, -1, 2, -2)]
    near += [at(z, ymod(y + r), c) for r in (1, 2, 3)] + [mate]
    xs = [{"hid": lax.rem(hid + k, 4)} for k in (1, 2, 3)]

    def stand_in(size):
        if size == int(size):
            return gsend.at[pl.ds(0, int(size))]
        return gsend.at[pl.ds(0, int(2 * size)), :, pl.ds(0, HALF)]

    slots = {}
    sent = {}

    def slot(table, key):
        return table.setdefault(key, len(table))

    def send(key, src, dst, dev, size=1, phase="w", plane=None):
        sent[phase, plane] = sent.get((phase, plane), 0) + size
        pltpu.make_async_remote_copy(
            src_ref=src, dst_ref=dst, send_sem=ssem.at[PHASES[phase]],
            recv_sem=rsem.at[slot(slots, key)], device_id=dev, device_id_type=MESH,
        ).start()

    def recv(key, size=1):
        part = stand_in(size)
        pltpu.make_async_remote_copy(
            src_ref=part, dst_ref=part, send_sem=ssem.at[0],
            recv_sem=rsem.at[slot(slots, key)], device_id=mate, device_id_type=MESH,
        ).wait_recv()

    loads = [
        pltpu.make_async_copy(src, dst, lsem.at[i]) for i, (src, dst) in enumerate((
            (up_ref, uf.at[z, y, c]), (down_ref, vf.at[z, y, c]), (wid_ref, wid_v),
            (tok_ref, rows_v.at[0]), (cot_ref, rows_v.at[1]),
        ))
    ]
    for copy in loads:
        copy.start()

    barrier = pltpu.get_barrier_semaphore()
    for dev in near + xs:
        pl.semaphore_signal(barrier, inc=1, device_id=dev, device_id_type=MESH)

    loads[0].wait()
    loads[1].wait()
    pl.semaphore_wait(barrier, len(near) + len(xs))

    def peer_y(r):
        return ymod(y + r)

    def u_share(k):
        zz = zmod(z + k)
        for r in (1, 3, 2):
            ref = uf.at[zz, y, c]
            send(("uy", k), ref, ref, at(z, peer_y(r), c))

    def u_direct(k):
        ref = uf.at[z, y, c]
        send(("uz", k), ref, ref, at(zmod(z + k), y, c))

    def u_pass(k):
        near, far, cols = (-1, -2, halves(1)) if k > 0 else (1, 2, halves(0))
        ref = uf.at[zmod(z + k), y, c]
        send(("uz", near - k), ref, ref, at(zmod(z + near), y, c))
        ref = uf.at[zmod(z + k), y, c, :, cols]
        send(("uz", 4), ref, ref, at(zmod(z + far), y, c), 0.5)

    def u_recv(k):
        recv(("uz", -k if k != 4 else 4))

    def u_group(k):
        recv(("uy", k), 3)
        zz = zmod(z + k)
        send("wc", uf.at[zz, :, c], uf.at[zz, :, c], mate, 4, "wc")

    def v_mate(r, k):
        ref = vf.at[zmod(z + k), peer_y(r), c]
        send("wc", ref, ref, mate, 1, "wc")

    def v_to(r, k, hop):
        ref = vf.at[zmod(z + k), peer_y(r), c]
        far = k - hop
        send(("vz", r, 4 if abs(far) == 4 else far), ref, ref, at(zmod(z + hop), y, c))

    def v_direct(r):
        for k in (1, -1, 2, -2):
            v_to(r, 0, k)

    def v_recv(r, k):
        recv(("vz", r, k))
        if abs(k) == 2:
            near = -1 if k > 0 else 1
            if (r < 2) == (k < 0):
                v_to(r, k, 2 * near)
            v_to(r, k, near)
        v_mate(r, k)

    own_v = vf.at[z, y, c]
    for r in (1, 3, 2):
        send(("vy", r), own_v, own_v, at(z, peer_y(r), c))
    v_direct(0)
    u_direct(1)
    u_direct(-1)
    u_share(0)
    u_direct(2)
    u_direct(-2)

    for copy in loads[2:]:
        copy.wait()
    wid = wid_v[...]
    level = lax.broadcasted_iota(jnp.int32, (8, ROWS), 0)
    ind = (jnp.broadcast_to(wid, (8, ROWS)) == level).astype(F32)
    ind16 = ind.astype(BF16)
    ia = lax.broadcasted_iota(jnp.int32, (ROWS, ROWS), 0)
    ib = lax.broadcasted_iota(jnp.int32, (ROWS, ROWS), 1)
    above = (ia < ib).astype(F32).astype(BF16)
    below = (ib < ia).astype(F32).astype(BF16)
    eye = (ia == ib).astype(F32).astype(BF16)
    counts = jnp.sum(ind, axis=1, keepdims=True)
    wider = [
        sum([counts[k:k + 1] for k in range(lo, 4)], jnp.zeros((1, 1), F32)) for lo in range(5)
    ]
    pre_row = jnp.dot(ind16, above, preferred_element_type=F32)
    pre_col = lax.dot_general(below, ind16, NT, preferred_element_type=F32)
    ind_col = lax.dot_general(eye, ind16, NT, preferred_element_type=F32)
    rank_row = sum([ind[k:k + 1] * (pre_row[k:k + 1] + wider[k + 1]) for k in range(4)])
    rank_col = sum(
        [ind_col[:, k:k + 1] * (pre_col[:, k:k + 1] + wider[k + 1]) for k in range(4)]
    )
    perm[...] = (ia == rank_row.astype(jnp.int32)).astype(F32).astype(BF16)
    permt[...] = (ib == rank_col.astype(jnp.int32)).astype(F32).astype(BF16)
    mine = pl.ds(pl.multiple_of(hid * COLS, COLS), COLS)
    for a in (0, 1):
        xg[a, :, mine] = jnp.dot(perm[...], rows_v[a], preferred_element_type=F32).astype(BF16)

    def xpart(h, lo, hi):
        return xg.at[:, pl.ds(lo, hi - lo), pl.ds(h * COLS, COLS)]

    def xsend(src, dst, h, lo, hi, key):
        part = xpart(h, lo, hi)
        send(key, part, part, xs[(dst - src) % 4 - 1], (hi - lo) // 32, "x", src)

    @pl.when(hid == 2)
    def _():
        xsend(2, 1, 2, 0, 128, "x0")
        xsend(2, 3, 2, 128, 256, "x0")
        xsend(2, 3, 2, 0, 64, "xm")
        xsend(2, 1, 2, 256, 384, "x1")
        xsend(2, 3, 2, 384, 512, "x1")

    @pl.when(hid == 1)
    def _():
        xsend(1, 0, 1, 0, 256, "x0")
        xsend(1, 2, 1, 0, 64, "xm")
        xsend(1, 3, 1, 0, 64, "xm")
        xsend(1, 0, 1, 256, 512, "x1")

    @pl.when(hid == 3)
    def _():
        xsend(3, 0, 3, 0, 256, "x0")
        xsend(3, 2, 3, 0, 64, "xm")
        xsend(3, 1, 3, 0, 128, "xm")
        xsend(3, 0, 3, 256, 512, "x1")

    @pl.when(hid == 0)
    def _():
        xsend(0, 1, 0, 0, 128, "xm")
        xsend(0, 3, 0, 0, 64, "xm")
        xsend(0, 2, 0, 0, 64, "xm")

    def forward_tokens(part):
        for plane, lo in ((1, 256 * part), (3, 256 * part + 128)):
            @pl.when(hid == plane)
            def _():
                recv(f"x{part}", 4)
                xsend(plane, 0, 2, lo, lo + 128, f"x{part}")

    for r in (3, 1, 2):
        recv(("vy", (4 - r) % 4))
        v_direct(r)
        v_mate(r, 0)
    v_mate(0, 0)
    for k in (1, -1):
        u_recv(k)
        u_share(k)
    for k in (2, -2):
        u_recv(k)
        u_pass(k)
        u_share(k)
    for k in (2, -2, 1, -1):
        v_recv(0, k)
    forward_tokens(0)
    for r in (3, 1, 2):
        for k in (2, -2, 1, -1):
            v_recv(r, k)
    for k in (3, -3, 4):
        u_recv(k)
        u_share(k)
    u_group(0)
    for k in (3, -3, 4):
        v_recv(0, k)
    u_group(1)
    u_group(-1)
    forward_tokens(1)
    u_group(2)
    u_group(-2)
    for r in (3, 1, 2):
        for k in (3, -3, 4):
            v_recv(r, k)
    u_group(3)
    u_group(-3)
    u_group(4)
    recv("wc", 64)

    def units(lo_row, n_row, lo_tile, hi_tile, count):
        rows = pl.ds(lo_row, n_row)

        def body(j, carry):
            cols = pl.ds(pl.multiple_of(j * TILE, TILE), TILE)
            u = uf[:, :, :, :, cols].reshape(D, TILE)
            v = vf[:, :, :, :, cols].reshape(D, TILE)
            pre = jnp.dot(xg[0, rows, :], u, preferred_element_type=F32)
            gh = jnp.dot(xg[1, rows, :], v, preferred_element_type=F32)
            act, slope = gelu_pair(pre)
            pg = gh * slope
            if count is not None:
                row = lax.broadcasted_iota(jnp.int32, (n_row, TILE), 0).astype(F32) + lo_row
                keep = row < count
                act = jnp.where(keep, act, 0.0)
                pg = jnp.where(keep, pg, 0.0)
            hbuf[rows, cols] = act.astype(BF16)
            pbuf[rows, cols] = pg.astype(BF16)
            return carry

        lax.fori_loop(lo_tile, hi_tile, body, 0, unroll=True)

    def outputs(plane, d, lo_row, n_row, n_unit):
        rows = pl.ds(lo_row, n_row)
        for a, val, w in ((0, hbuf, vf), (1, pbuf, uf)):
            wt = w[2 * d:2 * d + 2].reshape(COLS, UNITS)[:, :n_unit]
            out = lax.dot_general(val[rows, :n_unit], wt, NT, preferred_element_type=F32)
            if d == plane:
                ro[plane, a, rows, :] = out.astype(BF16)
            else:
                so[d, a, rows, :] = out.astype(BF16)

    def osend(src, dst, d, lo, hi, via=False):
        rows = pl.ds(lo, hi - lo)
        to = fo.at[:, rows, :] if via else ro.at[src, :, rows, :]
        send(f"f{lo // 256}" if via else "o", so.at[d, :, rows, :], to,
             xs[(dst - src) % 4 - 1], (hi - lo) // 32, "o", src)

    def tile(i):
        return lax.rem(lax.div(z, 2) + (2, 1, 3, 0)[i], 4)

    def grads(plane, n_row, h):
        hc = halves(h)
        for i in range(4):
            dt = tile(i)
            cols = pl.ds(pl.multiple_of(dt * COLS, COLS), COLS)
            zs = pl.ds(2 * dt, 2)
            for a, val in ((1, hbuf), (0, pbuf)):
                g = lax.dot_general(
                    xg[a, :n_row, cols], val[:n_row, hc], TN, preferred_element_type=F32)
                g = g.reshape(2, NY, 2, 16, HALF)
                lane[a, zs, :, :, hc] = jnp.where(c == 0, g[:, :, 0], g[:, :, 1])
                part = pl.ds(32 * a + 8 * dt, 8)
                other = jnp.where(c == 0, g[:, :, 1], g[:, :, 0]).astype(BF16)
                gsend[part, :, hc] = other.reshape(8, 16, HALF)
                send(("gc", h, a, GROUP[i]), gsend.at[part, :, hc], grecv.at[part, :, hc], mate,
                     4, "g", plane)

    def mate_grads(h, a, group):
        recv(("gc", h, a, group), 8 if group == 1 else 4)

    others = (
        (1, 128, 8, (0, 3, 2, 1)), (2, 64, 6, (0, 1, 3, 2)), (3, 64, 6, (1, 0, 2, 3)),
    )

    def row_outputs(lo, n_unit, dests=(2, 1, 3, 0)):
        for d in dests:
            outputs(0, d, lo, 256, n_unit)
            if d == 2:
                osend(0, 1, 2, lo, lo + 128, True)
                osend(0, 3, 2, lo + 128, lo + 256, True)
            elif d:
                osend(0, d, d, lo, lo + 256)

    @pl.when(hid == 0)
    def _():
        recv("x0", 24)
        units(0, 256, 2, 4, wider[1])
        grads(0, 256, 1)
        units(0, 256, 0, 2, None)

    for plane, n_row, n_in, dests in others:
        @pl.when(hid == plane)
        def _():
            recv("xm", n_in)
            count = wider[min(plane + 1, 3)]
            units(0, n_row, 2, 4, count)
            grads(plane, n_row, 1)
            units(0, n_row, 0, 2, count)
            for d in dests:
                outputs(plane, d, 0, n_row, UNITS)
                if d != plane:
                    osend(plane, d, d, 0, n_row)

    def rest_of_rows():
        @pl.when(hid == 0)
        def _():
            recv("x1", 24)
            row_outputs(0, UNITS, (2,))
            units(256, 256, 0, 2, None)
            row_outputs(0, UNITS, (1, 3))
            grads(0, 512, 0)
            row_outputs(0, UNITS, (0,))

        for plane, n_row, _, _ in others:
            @pl.when(hid == plane)
            def _():
                grads(plane, n_row, 0)

    def forward_outputs(part):
        for plane, lo in ((1, 256 * part), (3, 256 * part + 128)):
            @pl.when(hid == plane)
            def _():
                recv(f"f{part}", 4)
                rows = pl.ds(lo, 128)
                send("o", fo.at[:, rows, :], ro.at[0, :, rows, :], xs[(2 - plane) % 4 - 1], 4,
                     "o", plane)

    def total(h, a, zz, yy):
        hc = halves(h)
        return lane[a, zz, yy, :, hc] + grecv[32 * a + 4 * zz + yy, :, hc].astype(F32)

    def steps(p, d):
        return 4 if p == d else 3

    def ring(h, s):
        hc = halves(h)
        for p in (0, 1):
            for d in (0, 1):
                first = 4 - steps(p, d)
                ys = pl.ds(2 * p, 2)
                if s > first:
                    recv(("v", h, p, d, s - 1))
                if s < first:
                    continue
                zz = zmod(z + 4 - s) if d == 0 else zmod(z - 4 + s)
                for r in (2 * p, 2 * p + 1):
                    val = total(h, 1, zz, peer_y(r))
                    if s > first:
                        val = val + rv[d, s - 1, r, :, hc].astype(F32)
                    sv[d, s, r, :, hc] = val.astype(BF16)
                send(("v", h, p, d, s), sv.at[d, s, ys, :, hc], rv.at[d, s, ys, :, hc],
                     zp if d == 0 else zm, 1, "r")

    def ring_end(h):
        hc = halves(h)
        for p in (1, 0):
            for d in (0, 1):
                recv(("v", h, p, d, 3))
            for r in (2 * p + 1, 2 * p):
                val = total(h, 1, z, peer_y(r))
                for d in (0, 1):
                    val = val + rv[d, 3, r, :, hc].astype(F32)
                if r:
                    svy[r, :, hc] = val.astype(BF16)
                    send(("vw", h), svy.at[r, :, hc], rvy.at[r, :, hc], at(z, peer_y(r), c),
                         0.5, "r")
                else:
                    vz[:, hc] = val

    def up_share(h, k):
        hc = halves(h)
        for r in (1, 3, 2):
            su1[k + 3, r, :, hc] = total(h, 0, zmod(z + k), peer_y(r)).astype(BF16)
            send(("uu", h, k), su1.at[k + 3, r, :, hc], ru1.at[k + 3, r, :, hc],
                 at(z, peer_y(r), c), 0.5, "r")

    def up_sum(h, k):
        hc = halves(h)
        val = total(h, 0, zmod(z + k), y)
        recv(("uu", h, k), 1.5)
        for r in (1, 3, 2):
            val = val + ru1[k + 3, r, :, hc].astype(F32)
        return val

    def up_send(h, k, val, key, hop):
        hc = halves(h)
        suz[k + 3, :, hc] = val.astype(BF16)
        send(key, suz.at[k + 3, :, hc], ruz.at[k + 3, :, hc], at(zmod(z + hop), y, c), 0.5, "r")

    def up_far(h):
        up_send(h, 4, up_sum(h, 4), ("uf", h, 4), 2 if h == 0 else -2)
        up_send(h, 3, up_sum(h, 3), ("uf", h, 3), 1)
        up_send(h, -3, up_sum(h, -3), ("uf", h, -3), -1)

    def up_near(h):
        for k in (1, -1):
            up_send(h, k, up_sum(h, k), ("ue", h), k)

    def up_two(h):
        hc = halves(h)
        for k, far in ((2, 3), (-2, -3)):
            val = up_sum(h, k)
            recv(("uf", h, far), 0.5)
            val = val + ruz[far + 3, :, hc].astype(F32)
            if (k == 2) == (h == 0):
                recv(("uf", h, 4), 0.5)
                val = val + ruz[7, :, hc].astype(F32)
            up_send(h, k, val, ("ue", h), k)

    def start_half(h):
        mate_grads(h, 1, 0)
        ring(h, 0)
        mate_grads(h, 0, 0)
        up_share(h, 4)
        mate_grads(h, 0, 1)
        for k in (3, -3, 2, -2):
            up_share(h, k)
        mate_grads(h, 0, 2)
        for k in (1, -1, 0):
            up_share(h, k)
        mate_grads(h, 1, 1)
        mate_grads(h, 1, 2)

    start_half(1)
    rest_of_rows()
    start_half(0)
    ring(1, 1)
    up_far(1)

    @pl.when(hid == 0)
    def _():
        row_outputs(256, HALF)

    ring(0, 1)
    ring(1, 2)
    up_near(1)
    up_far(0)
    forward_outputs(0)
    ring(0, 2)
    ring(1, 3)
    up_two(1)
    up_near(0)
    ring(0, 3)
    ring_end(1)
    uy[:, halves(1)] = up_sum(1, 0)
    up_two(0)
    forward_outputs(1)
    uy[:, halves(0)] = up_sum(0, 0)
    ring_end(0)

    for plane, n_in in ((0, 8), (1, 20), (2, 22), (3, 22)):
        @pl.when(hid == plane)
        def _():
            recv("o", n_in)

    for a, ref in ((0, mixed_ref), (1, gtok_ref)):
        top = ro[0, a, 0:128].astype(F32) + ro[1, a, 0:128].astype(F32)
        wide = top[:64] + ro[2, a, 0:64].astype(F32) + ro[3, a, 0:64].astype(F32)
        ro[0, a, 0:128] = jnp.concatenate([wide, top[64:]], axis=0).astype(BF16)
        ref[...] = jnp.dot(permt[...], ro[0, a], preferred_element_type=F32).astype(BF16)

    for h in (1, 0):
        hc = halves(h)
        recv(("vw", h), 1.5)
        val = vz[:, hc]
        for r in (1, 3, 2):
            val = val + rvy[r, :, hc].astype(F32)
        gdown_ref[:, hc] = val
        recv(("ue", h), 2)
        val = uy[:, hc]
        for k in (1, -1, 2, -2):
            val = val + ruz[k + 3, :, hc].astype(F32)
        gup_ref[:, hc] = val

    def left(phase, plane):
        part = stand_in(sent[phase, plane])
        pltpu.make_async_remote_copy(
            src_ref=part, dst_ref=part, send_sem=ssem.at[PHASES[phase]], recv_sem=rsem.at[0],
            device_id=mate, device_id_type=MESH,
        ).wait_send()

    for phase in ("w", "wc", "r"):
        left(phase, None)
    for plane in range(4):
        @pl.when(hid == plane)
        def _():
            for phase in ("x", "o", "g"):
                left(phase, plane)
    assert len(slots) == N_SEM, len(slots)


def store(*refs):
    sem = refs[-1]
    copies = [pltpu.make_async_copy(refs[i], refs[4 + i], sem.at[i]) for i in range(4)]
    for copy in copies:
        copy.start()
    for copy in copies:
        copy.wait()


def per_device(tokens, width_index, up_weight, down_weight, cotangent):
    vm = pl.BlockSpec(memory_space=pltpu.VMEM)
    hbm = pl.BlockSpec(memory_space=pltpu.HBM)
    block = (16, UNITS)
    shapes = [((ROWS, COLS), BF16), ((ROWS, COLS), BF16), (block, F32), (block, F32)]

    def buf(*shape):
        return pltpu.VMEM(shape, BF16)

    results = pl.pallas_call(
        kernel,
        out_shape=tuple(pltpu.VMEM(*shape) for shape in shapes),
        in_specs=[hbm] * 5,
        out_specs=(vm,) * 4,
        scratch_shapes=[
            buf(NZ, NY, 2, *block), buf(NZ, NY, 2, *block),
            buf(2, ROWS, D), buf(ROWS, UNITS), buf(ROWS, UNITS),
            buf(4, 2, ROWS, COLS), buf(4, 2, ROWS, COLS), buf(2, ROWS, COLS),
            buf(ROWS, ROWS), buf(ROWS, ROWS),
            buf(64, *block), buf(64, *block),
            pltpu.VMEM((2, NZ, NY, *block), F32),
            buf(2, ROWS, COLS), pltpu.VMEM((1, ROWS), jnp.int32),
            buf(2, 4, NY, *block), buf(2, 4, NY, *block),
            buf(NZ, NY, *block), buf(NZ, NY, *block),
            buf(NZ, *block), buf(NZ, *block),
            buf(NY, *block), buf(NY, *block),
            pltpu.VMEM(block, F32), pltpu.VMEM(block, F32),
            pltpu.SemaphoreType.DMA((len(PHASES),)), pltpu.SemaphoreType.DMA((N_SEM,)),
            pltpu.SemaphoreType.DMA((5,)),
        ],
        compiler_params=pltpu.CompilerParams(
            collective_id=0, has_side_effects=True, vmem_limit_bytes=48 * 1024 * 1024,
        ),
    )(*[
        pltpu.with_memory_space_constraint(x, pltpu.HBM)
        for x in (tokens, width_index.reshape(1, ROWS), up_weight, down_weight.T, cotangent)
    ])
    mixed, gtok, gup, gdown = pl.pallas_call(
        store,
        out_shape=tuple(jax.ShapeDtypeStruct(*shape) for shape in shapes),
        in_specs=[vm] * 4,
        out_specs=(hbm,) * 4,
        scratch_shapes=[pltpu.SemaphoreType.DMA((4,))],
    )(*[pltpu.with_memory_space_constraint(x, pltpu.VMEM) for x in results])
    return mixed, gtok, gup, gdown.T


def solution(mesh):
    placed = (P("tok", "hid"), P("tok"), P("tok", "hid"), P("hid", "tok"), P("tok", "hid"))
    return jax.shard_map(
        per_device,
        mesh=mesh,
        in_specs=placed,
        out_specs=(P("tok", "hid"), P("tok", "hid"), P("tok", "hid"), P("hid", "tok")),
        check_vma=False,
    )
```

```python
import jax
import jax.numpy as jnp
from jax import lax
from jax.experimental import pallas as pl
from jax.experimental.pallas import tpu as pltpu
from jax.sharding import PartitionSpec as P

root_half = 0.7071067811865476
inv_root_tau = 0.3989422804014327
F32 = jnp.float32
BF16 = jnp.bfloat16
MESH = pl.DeviceIdType.MESH

ROWS = 512
COLS = 256
D = 1024
UNITS = 1024
NZ, NY = 8, 4
TILE = 256
HALF = 512
N_SEM = 119
GROUP = (0, 1, 1, 2)
PHASES = dict(w=0, wc=1, x=2, o=3, g=4, r=5)

NT = (((1,), (1,)), ((), ()))
TN = (((0,), (0,)), ((), ()))


def gelu_pair(pre_act):
    cumul = 0.5 * (1.0 + lax.erf(pre_act * root_half))
    return (pre_act * cumul, cumul + pre_act * jnp.exp(-0.5 * pre_act * pre_act) * inv_root_tau)


def kernel(
    tok_ref, wid_ref, up_ref, down_ref, cot_ref,
    mixed_ref, gtok_ref, gup_ref, gdown_ref,
    uf, vf, xg, hbuf, pbuf, so, ro, fo, perm, permt,
    gsend, grecv, lane, rows_v, wid_v,
    sv, rv, su1, ru1, suz, ruz, svy, rvy, uy, vz,
    ssem, rsem, lsem,
):
    hid = lax.axis_index("hid")
    tok = lax.axis_index("tok")
    c = lax.rem(tok, 2)
    y = lax.rem(lax.div(tok, 2), NY)
    z = lax.div(tok, 2 * NY)

    def zmod(v):
        return lax.rem(v + 2 * NZ, NZ)

    def ymod(v):
        return lax.rem(v + 2 * NY, NY)

    def halves(h):
        return pl.ds(HALF * h, HALF)

    def at(zz, yy, cc):
        return {"tok": (zz * NY + yy) * 2 + cc}

    zp, zm = at(zmod(z + 1), y, c), at(zmod(z - 1), y, c)
    mate = at(z, y, 1 - c)
    near = [at(zmod(z + k), y, c) for k in (1, -1, 2, -2)]
    near += [at(z, ymod(y + r), c) for r in (1, 2, 3)] + [mate]
    xs = [{"hid": lax.rem(hid + k, 4)} for k in (1, 2, 3)]

    def stand_in(size):
        if size == int(size):
            return gsend.at[pl.ds(0, int(size))]
        return gsend.at[pl.ds(0, int(2 * size)), :, pl.ds(0, HALF)]

    slots = {}
    sent = {}

    def slot(table, key):
        return table.setdefault(key, len(table))

    def send(key, src, dst, dev, size=1, phase="w", plane=None):
        sent[phase, plane] = sent.get((phase, plane), 0) + size
        pltpu.make_async_remote_copy(
            src_ref=src, dst_ref=dst, send_sem=ssem.at[PHASES[phase]],
            recv_sem=rsem.at[slot(slots, key)], device_id=dev, device_id_type=MESH,
        ).start()

    def recv(key, size=1):
        part = stand_in(size)
        pltpu.make_async_remote_copy(
            src_ref=part, dst_ref=part, send_sem=ssem.at[0],
            recv_sem=rsem.at[slot(slots, key)], device_id=mate, device_id_type=MESH,
        ).wait_recv()

    loads = [
        pltpu.make_async_copy(src, dst, lsem.at[i]) for i, (src, dst) in enumerate((
            (up_ref, uf.at[z, y, c]), (down_ref, vf.at[z, y, c]), (wid_ref, wid_v),
            (tok_ref, rows_v.at[0]), (cot_ref, rows_v.at[1]),
        ))
    ]
    for copy in loads:
        copy.start()

    barrier = pltpu.get_barrier_semaphore()
    for dev in near + xs:
        pl.semaphore_signal(barrier, inc=1, device_id=dev, device_id_type=MESH)

    loads[0].wait()
    loads[1].wait()
    pl.semaphore_wait(barrier, len(near) + len(xs))

    def peer_y(r):
        return ymod(y + r)

    def u_share(k):
        zz = zmod(z + k)
        for r in (1, 3, 2):
            ref = uf.at[zz, y, c]
            send(("uy", k), ref, ref, at(z, peer_y(r), c))

    def u_direct(k):
        ref = uf.at[z, y, c]
        send(("uz", k), ref, ref, at(zmod(z + k), y, c))

    def u_pass(k):
        near, far, cols = (-1, -2, halves(1)) if k > 0 else (1, 2, halves(0))
        ref = uf.at[zmod(z + k), y, c]
        send(("uz", near - k), ref, ref, at(zmod(z + near), y, c))
        ref = uf.at[zmod(z + k), y, c, :, cols]
        send(("uz", 4), ref, ref, at(zmod(z + far), y, c), 0.5)

    def u_recv(k):
        recv(("uz", -k if k != 4 else 4))

    def u_group(k):
        recv(("uy", k), 3)
        zz = zmod(z + k)
        send("wc", uf.at[zz, :, c], uf.at[zz, :, c], mate, 4, "wc")

    def v_mate(r, k):
        ref = vf.at[zmod(z + k), peer_y(r), c]
        send("wc", ref, ref, mate, 1, "wc")

    def v_to(r, k, hop):
        ref = vf.at[zmod(z + k), peer_y(r), c]
        far = k - hop
        send(("vz", r, 4 if abs(far) == 4 else far), ref, ref, at(zmod(z + hop), y, c))

    def v_direct(r):
        for k in (1, -1, 2, -2):
            v_to(r, 0, k)

    def v_recv(r, k):
        recv(("vz", r, k))
        if abs(k) == 2:
            near = -1 if k > 0 else 1
            if (r < 2) == (k < 0):
                v_to(r, k, 2 * near)
            v_to(r, k, near)
        v_mate(r, k)

    own_v = vf.at[z, y, c]
    for r in (1, 3, 2):
        send(("vy", r), own_v, own_v, at(z, peer_y(r), c))
    v_direct(0)
    u_direct(1)
    u_direct(-1)
    u_share(0)
    u_direct(2)
    u_direct(-2)

    for copy in loads[2:]:
        copy.wait()
    wid = wid_v[...]
    level = lax.broadcasted_iota(jnp.int32, (8, ROWS), 0)
    ind = (jnp.broadcast_to(wid, (8, ROWS)) == level).astype(F32)
    ind16 = ind.astype(BF16)
    ia = lax.broadcasted_iota(jnp.int32, (ROWS, ROWS), 0)
    ib = lax.broadcasted_iota(jnp.int32, (ROWS, ROWS), 1)
    above = (ia < ib).astype(F32).astype(BF16)
    below = (ib < ia).astype(F32).astype(BF16)
    eye = (ia == ib).astype(F32).astype(BF16)
    counts = jnp.sum(ind, axis=1, keepdims=True)
    wider = [
        sum([counts[k:k + 1] for k in range(lo, 4)], jnp.zeros((1, 1), F32)) for lo in range(5)
    ]
    pre_row = jnp.dot(ind16, above, preferred_element_type=F32)
    pre_col = lax.dot_general(below, ind16, NT, preferred_element_type=F32)
    ind_col = lax.dot_general(eye, ind16, NT, preferred_element_type=F32)
    rank_row = sum([ind[k:k + 1] * (pre_row[k:k + 1] + wider[k + 1]) for k in range(4)])
    rank_col = sum(
        [ind_col[:, k:k + 1] * (pre_col[:, k:k + 1] + wider[k + 1]) for k in range(4)]
    )
    perm[...] = (ia == rank_row.astype(jnp.int32)).astype(F32).astype(BF16)
    permt[...] = (ib == rank_col.astype(jnp.int32)).astype(F32).astype(BF16)
    mine = pl.ds(pl.multiple_of(hid * COLS, COLS), COLS)
    for a in (0, 1):
        xg[a, :, mine] = jnp.dot(perm[...], rows_v[a], preferred_element_type=F32).astype(BF16)

    def xpart(h, lo, hi):
        return xg.at[:, pl.ds(lo, hi - lo), pl.ds(h * COLS, COLS)]

    def xsend(src, dst, h, lo, hi, key):
        part = xpart(h, lo, hi)
        send(key, part, part, xs[(dst - src) % 4 - 1], (hi - lo) // 32, "x", src)

    @pl.when(hid == 2)
    def _():
        xsend(2, 1, 2, 0, 128, "x0")
        xsend(2, 3, 2, 128, 256, "x0")
        xsend(2, 3, 2, 0, 64, "xm")
        xsend(2, 1, 2, 256, 384, "x1")
        xsend(2, 3, 2, 384, 512, "x1")

    @pl.when(hid == 1)
    def _():
        xsend(1, 0, 1, 0, 256, "x0")
        xsend(1, 2, 1, 0, 64, "xm")
        xsend(1, 3, 1, 0, 64, "xm")
        xsend(1, 0, 1, 256, 512, "x1")

    @pl.when(hid == 3)
    def _():
        xsend(3, 0, 3, 0, 256, "x0")
        xsend(3, 2, 3, 0, 64, "xm")
        xsend(3, 1, 3, 0, 128, "xm")
        xsend(3, 0, 3, 256, 512, "x1")

    @pl.when(hid == 0)
    def _():
        xsend(0, 1, 0, 0, 128, "xm")
        xsend(0, 3, 0, 0, 64, "xm")
        xsend(0, 2, 0, 0, 64, "xm")

    def forward_tokens(part):
        for plane, lo in ((1, 256 * part), (3, 256 * part + 128)):
            @pl.when(hid == plane)
            def _():
                recv(f"x{part}", 4)
                xsend(plane, 0, 2, lo, lo + 128, f"x{part}")

    for r in (3, 1, 2):
        recv(("vy", (4 - r) % 4))
        v_direct(r)
        v_mate(r, 0)
    v_mate(0, 0)
    for k in (1, -1):
        u_recv(k)
        u_share(k)
    for k in (2, -2):
        u_recv(k)
        u_pass(k)
        u_share(k)
    for k in (2, -2, 1, -1):
        v_recv(0, k)
    forward_tokens(0)
    for r in (3, 1, 2):
        for k in (2, -2, 1, -1):
            v_recv(r, k)
    for k in (3, -3, 4):
        u_recv(k)
        u_share(k)
    u_group(0)
    for k in (3, -3, 4):
        v_recv(0, k)
    u_group(1)
    u_group(-1)
    forward_tokens(1)
    u_group(2)
    u_group(-2)
    for r in (3, 1, 2):
        for k in (3, -3, 4):
            v_recv(r, k)
    u_group(3)
    u_group(-3)
    u_group(4)
    recv("wc", 64)

    def units(lo_row, n_row, lo_tile, hi_tile, count):
        rows = pl.ds(lo_row, n_row)

        def body(j, carry):
            cols = pl.ds(pl.multiple_of(j * TILE, TILE), TILE)
            u = uf[:, :, :, :, cols].reshape(D, TILE)
            v = vf[:, :, :, :, cols].reshape(D, TILE)
            pre = jnp.dot(xg[0, rows, :], u, preferred_element_type=F32)
            gh = jnp.dot(xg[1, rows, :], v, preferred_element_type=F32)
            act, slope = gelu_pair(pre)
            pg = gh * slope
            if count is not None:
                row = lax.broadcasted_iota(jnp.int32, (n_row, TILE), 0).astype(F32) + lo_row
                keep = row < count
                act = jnp.where(keep, act, 0.0)
                pg = jnp.where(keep, pg, 0.0)
            hbuf[rows, cols] = act.astype(BF16)
            pbuf[rows, cols] = pg.astype(BF16)
            return carry

        lax.fori_loop(lo_tile, hi_tile, body, 0, unroll=True)

    def outputs(plane, d, lo_row, n_row, n_unit):
        rows = pl.ds(lo_row, n_row)
        for a, val, w in ((0, hbuf, vf), (1, pbuf, uf)):
            wt = w[2 * d:2 * d + 2].reshape(COLS, UNITS)[:, :n_unit]
            out = lax.dot_general(val[rows, :n_unit], wt, NT, preferred_element_type=F32)
            if d == plane:
                ro[plane, a, rows, :] = out.astype(BF16)
            else:
                so[d, a, rows, :] = out.astype(BF16)

    def osend(src, dst, d, lo, hi, via=False):
        rows = pl.ds(lo, hi - lo)
        to = fo.at[:, rows, :] if via else ro.at[src, :, rows, :]
        send(f"f{lo // 256}" if via else "o", so.at[d, :, rows, :], to,
             xs[(dst - src) % 4 - 1], (hi - lo) // 32, "o", src)

    def tile(i):
        return lax.rem(lax.div(z, 2) + (2, 1, 3, 0)[i], 4)

    def grads(plane, n_row, h):
        hc = halves(h)
        for i in range(4):
            dt = tile(i)
            cols = pl.ds(pl.multiple_of(dt * COLS, COLS), COLS)
            zs = pl.ds(2 * dt, 2)
            for a, val in ((1, hbuf), (0, pbuf)):
                g = lax.dot_general(
                    xg[a, :n_row, cols], val[:n_row, hc], TN, preferred_element_type=F32)
                g = g.reshape(2, NY, 2, 16, HALF)
                lane[a, zs, :, :, hc] = jnp.where(c == 0, g[:, :, 0], g[:, :, 1])
                part = pl.ds(32 * a + 8 * dt, 8)
                other = jnp.where(c == 0, g[:, :, 1], g[:, :, 0]).astype(BF16)
                gsend[part, :, hc] = other.reshape(8, 16, HALF)
                send(("gc", h, a, GROUP[i]), gsend.at[part, :, hc], grecv.at[part, :, hc], mate,
                     4, "g", plane)

    def mate_grads(h, a, group):
        recv(("gc", h, a, group), 8 if group == 1 else 4)

    others = (
        (1, 128, 8, (0, 3, 2, 1)), (2, 64, 6, (0, 1, 3, 2)), (3, 64, 6, (1, 0, 2, 3)),
    )

    def row_outputs(lo, n_unit, dests=(2, 1, 3, 0)):
        for d in dests:
            outputs(0, d, lo, 256, n_unit)
            if d == 2:
                osend(0, 1, 2, lo, lo + 128, True)
                osend(0, 3, 2, lo + 128, lo + 256, True)
            elif d:
                osend(0, d, d, lo, lo + 256)

    @pl.when(hid == 0)
    def _():
        recv("x0", 24)
        units(0, 256, 2, 4, wider[1])
        grads(0, 256, 1)
        units(0, 256, 0, 2, None)
        row_outputs(0, UNITS, (2,))

    for plane, n_row, n_in, dests in others:
        @pl.when(hid == plane)
        def _():
            recv("xm", n_in)
            count = wider[min(plane + 1, 3)]
            units(0, n_row, 2, 4, count)
            grads(plane, n_row, 1)
            units(0, n_row, 0, 2, count)
            for d in dests:
                outputs(plane, d, 0, n_row, UNITS)
                if d != plane:
                    osend(plane, d, d, 0, n_row)

    def rest_of_rows():
        @pl.when(hid == 0)
        def _():
            recv("x1", 24)
            units(256, 256, 0, 2, None)
            row_outputs(0, UNITS, (1, 3))
            grads(0, 512, 0)
            row_outputs(0, UNITS, (0,))

        for plane, n_row, _, _ in others:
            @pl.when(hid == plane)
            def _():
                grads(plane, n_row, 0)

    def forward_outputs(part):
        for plane, lo in ((1, 256 * part), (3, 256 * part + 128)):
            @pl.when(hid == plane)
            def _():
                recv(f"f{part}", 4)
                rows = pl.ds(lo, 128)
                send("o", fo.at[:, rows, :], ro.at[0, :, rows, :], xs[(2 - plane) % 4 - 1], 4,
                     "o", plane)

    def total(h, a, zz, yy):
        hc = halves(h)
        return lane[a, zz, yy, :, hc] + grecv[32 * a + 4 * zz + yy, :, hc].astype(F32)

    def steps(p, d):
        return 4 if p == d else 3

    def ring(h, s):
        hc = halves(h)
        for p in (0, 1):
            for d in (0, 1):
                first = 4 - steps(p, d)
                ys = pl.ds(2 * p, 2)
                if s > first:
                    recv(("v", h, p, d, s - 1))
                if s < first:
                    continue
                zz = zmod(z + 4 - s) if d == 0 else zmod(z - 4 + s)
                for r in (2 * p, 2 * p + 1):
                    val = total(h, 1, zz, peer_y(r))
                    if s > first:
                        val = val + rv[d, s - 1, r, :, hc].astype(F32)
                    sv[d, s, r, :, hc] = val.astype(BF16)
                send(("v", h, p, d, s), sv.at[d, s, ys, :, hc], rv.at[d, s, ys, :, hc],
                     zp if d == 0 else zm, 1, "r")

    def ring_end(h):
        hc = halves(h)
        for p in (1, 0):
            for d in (0, 1):
                recv(("v", h, p, d, 3))
            for r in (2 * p + 1, 2 * p):
                val = total(h, 1, z, peer_y(r))
                for d in (0, 1):
                    val = val + rv[d, 3, r, :, hc].astype(F32)
                if r:
                    svy[r, :, hc] = val.astype(BF16)
                    send(("vw", h), svy.at[r, :, hc], rvy.at[r, :, hc], at(z, peer_y(r), c),
                         0.5, "r")
                else:
                    vz[:, hc] = val

    def up_share(h, k):
        hc = halves(h)
        for r in (1, 3, 2):
            su1[k + 3, r, :, hc] = total(h, 0, zmod(z + k), peer_y(r)).astype(BF16)
            send(("uu", h, k), su1.at[k + 3, r, :, hc], ru1.at[k + 3, r, :, hc],
                 at(z, peer_y(r), c), 0.5, "r")

    def up_sum(h, k):
        hc = halves(h)
        val = total(h, 0, zmod(z + k), y)
        recv(("uu", h, k), 1.5)
        for r in (1, 3, 2):
            val = val + ru1[k + 3, r, :, hc].astype(F32)
        return val

    def up_send(h, k, val, key, hop):
        hc = halves(h)
        suz[k + 3, :, hc] = val.astype(BF16)
        send(key, suz.at[k + 3, :, hc], ruz.at[k + 3, :, hc], at(zmod(z + hop), y, c), 0.5, "r")

    def up_far(h):
        up_send(h, 4, up_sum(h, 4), ("uf", h, 4), 2 if h == 0 else -2)
        up_send(h, 3, up_sum(h, 3), ("uf", h, 3), 1)
        up_send(h, -3, up_sum(h, -3), ("uf", h, -3), -1)

    def up_near(h):
        for k in (1, -1):
            up_send(h, k, up_sum(h, k), ("ue", h), k)

    def up_two(h):
        hc = halves(h)
        for k, far in ((2, 3), (-2, -3)):
            val = up_sum(h, k)
            recv(("uf", h, far), 0.5)
            val = val + ruz[far + 3, :, hc].astype(F32)
            if (k == 2) == (h == 0):
                recv(("uf", h, 4), 0.5)
                val = val + ruz[7, :, hc].astype(F32)
            up_send(h, k, val, ("ue", h), k)

    def start_half(h):
        mate_grads(h, 1, 0)
        ring(h, 0)
        mate_grads(h, 0, 0)
        up_share(h, 4)
        mate_grads(h, 0, 1)
        for k in (3, -3, 2, -2):
            up_share(h, k)
        mate_grads(h, 0, 2)
        for k in (1, -1, 0):
            up_share(h, k)
        mate_grads(h, 1, 1)
        mate_grads(h, 1, 2)

    start_half(1)
    rest_of_rows()
    start_half(0)
    ring(1, 1)
    up_far(1)

    @pl.when(hid == 0)
    def _():
        row_outputs(256, HALF)

    ring(0, 1)
    ring(1, 2)
    up_near(1)
    up_far(0)
    forward_outputs(0)
    ring(0, 2)
    ring(1, 3)
    up_two(1)
    up_near(0)
    ring(0, 3)
    ring_end(1)
    uy[:, halves(1)] = up_sum(1, 0)
    up_two(0)
    forward_outputs(1)
    uy[:, halves(0)] = up_sum(0, 0)
    ring_end(0)

    for plane, n_in in ((0, 8), (1, 20), (2, 22), (3, 22)):
        @pl.when(hid == plane)
        def _():
            recv("o", n_in)

    for a, ref in ((0, mixed_ref), (1, gtok_ref)):
        top = ro[0, a, 0:128].astype(F32) + ro[1, a, 0:128].astype(F32)
        wide = top[:64] + ro[2, a, 0:64].astype(F32) + ro[3, a, 0:64].astype(F32)
        ro[0, a, 0:128] = jnp.concatenate([wide, top[64:]], axis=0).astype(BF16)
        ref[...] = jnp.dot(permt[...], ro[0, a], preferred_element_type=F32).astype(BF16)

    for h in (1, 0):
        hc = halves(h)
        recv(("vw", h), 1.5)
        val = vz[:, hc]
        for r in (1, 3, 2):
            val = val + rvy[r, :, hc].astype(F32)
        gdown_ref[:, hc] = val
        recv(("ue", h), 2)
        val = uy[:, hc]
        for k in (1, -1, 2, -2):
            val = val + ruz[k + 3, :, hc].astype(F32)
        gup_ref[:, hc] = val

    def left(phase, plane):
        part = stand_in(sent[phase, plane])
        pltpu.make_async_remote_copy(
            src_ref=part, dst_ref=part, send_sem=ssem.at[PHASES[phase]], recv_sem=rsem.at[0],
            device_id=mate, device_id_type=MESH,
        ).wait_send()

    for phase in ("w", "wc", "r"):
        left(phase, None)
    for plane in range(4):
        @pl.when(hid == plane)
        def _():
            for phase in ("x", "o", "g"):
                left(phase, plane)
    assert len(slots) == N_SEM, len(slots)


def store(*refs):
    sem = refs[-1]
    copies = [pltpu.make_async_copy(refs[i], refs[4 + i], sem.at[i]) for i in range(4)]
    for copy in copies:
        copy.start()
    for copy in copies:
        copy.wait()


def per_device(tokens, width_index, up_weight, down_weight, cotangent):
    vm = pl.BlockSpec(memory_space=pltpu.VMEM)
    hbm = pl.BlockSpec(memory_space=pltpu.HBM)
    block = (16, UNITS)
    shapes = [((ROWS, COLS), BF16), ((ROWS, COLS), BF16), (block, F32), (block, F32)]

    def buf(*shape):
        return pltpu.VMEM(shape, BF16)

    results = pl.pallas_call(
        kernel,
        out_shape=tuple(pltpu.VMEM(*shape) for shape in shapes),
        in_specs=[hbm] * 5,
        out_specs=(vm,) * 4,
        scratch_shapes=[
            buf(NZ, NY, 2, *block), buf(NZ, NY, 2, *block),
            buf(2, ROWS, D), buf(ROWS, UNITS), buf(ROWS, UNITS),
            buf(4, 2, ROWS, COLS), buf(4, 2, ROWS, COLS), buf(2, ROWS, COLS),
            buf(ROWS, ROWS), buf(ROWS, ROWS),
            buf(64, *block), buf(64, *block),
            pltpu.VMEM((2, NZ, NY, *block), F32),
            buf(2, ROWS, COLS), pltpu.VMEM((1, ROWS), jnp.int32),
            buf(2, 4, NY, *block), buf(2, 4, NY, *block),
            buf(NZ, NY, *block), buf(NZ, NY, *block),
            buf(NZ, *block), buf(NZ, *block),
            buf(NY, *block), buf(NY, *block),
            pltpu.VMEM(block, F32), pltpu.VMEM(block, F32),
            pltpu.SemaphoreType.DMA((len(PHASES),)), pltpu.SemaphoreType.DMA((N_SEM,)),
            pltpu.SemaphoreType.DMA((5,)),
        ],
        compiler_params=pltpu.CompilerParams(
            collective_id=0, has_side_effects=True, vmem_limit_bytes=48 * 1024 * 1024,
        ),
    )(*[
        pltpu.with_memory_space_constraint(x, pltpu.HBM)
        for x in (tokens, width_index.reshape(1, ROWS), up_weight, down_weight.T, cotangent)
    ])
    mixed, gtok, gup, gdown = pl.pallas_call(
        store,
        out_shape=tuple(jax.ShapeDtypeStruct(*shape) for shape in shapes),
        in_specs=[vm] * 4,
        out_specs=(hbm,) * 4,
        scratch_shapes=[pltpu.SemaphoreType.DMA((4,))],
    )(*[pltpu.with_memory_space_constraint(x, pltpu.VMEM) for x in results])
    return mixed, gtok, gup, gdown.T


def solution(mesh):
    placed = (P("tok", "hid"), P("tok"), P("tok", "hid"), P("hid", "tok"), P("tok", "hid"))
    return jax.shard_map(
        per_device,
        mesh=mesh,
        in_specs=placed,
        out_specs=(P("tok", "hid"), P("tok", "hid"), P("tok", "hid"), P("hid", "tok")),
        check_vma=False,
    )
```

```python
import jax
import jax.numpy as jnp
from jax import lax
from jax.experimental import pallas as pl
from jax.experimental.pallas import tpu as pltpu
from jax.sharding import PartitionSpec as P

root_half = 0.7071067811865476
inv_root_tau = 0.3989422804014327
F32 = jnp.float32
BF16 = jnp.bfloat16
MESH = pl.DeviceIdType.MESH

ROWS = 512
COLS = 256
D = 1024
UNITS = 1024
NZ, NY = 8, 4
TILE = 256
HALF = 512
N_SEM = 119
GROUP = (0, 1, 1, 2)
PHASES = dict(w=0, wc=1, x=2, o=3, g=4, r=5)

NT = (((1,), (1,)), ((), ()))
TN = (((0,), (0,)), ((), ()))


def gelu_pair(pre_act):
    cumul = 0.5 * (1.0 + lax.erf(pre_act * root_half))
    return (pre_act * cumul, cumul + pre_act * jnp.exp(-0.5 * pre_act * pre_act) * inv_root_tau)


def kernel(
    tok_ref, wid_ref, up_ref, down_ref, cot_ref,
    mixed_ref, gtok_ref, gup_ref, gdown_ref,
    uf, vf, xg, hbuf, pbuf, so, ro, fo, perm, permt,
    gsend, grecv, lane, rows_v, wid_v,
    sv, rv, su1, ru1, suz, ruz, svy, rvy, uy, vz,
    ssem, rsem, lsem,
):
    hid = lax.axis_index("hid")
    tok = lax.axis_index("tok")
    c = lax.rem(tok, 2)
    y = lax.rem(lax.div(tok, 2), NY)
    z = lax.div(tok, 2 * NY)

    def zmod(v):
        return lax.rem(v + 2 * NZ, NZ)

    def ymod(v):
        return lax.rem(v + 2 * NY, NY)

    def halves(h):
        return pl.ds(HALF * h, HALF)

    def at(zz, yy, cc):
        return {"tok": (zz * NY + yy) * 2 + cc}

    zp, zm = at(zmod(z + 1), y, c), at(zmod(z - 1), y, c)
    mate = at(z, y, 1 - c)
    near = [at(zmod(z + k), y, c) for k in (1, -1, 2, -2)]
    near += [at(z, ymod(y + r), c) for r in (1, 2, 3)] + [mate]
    xs = [{"hid": lax.rem(hid + k, 4)} for k in (1, 2, 3)]

    def stand_in(size):
        if size == int(size):
            return gsend.at[pl.ds(0, int(size))]
        return gsend.at[pl.ds(0, int(2 * size)), :, pl.ds(0, HALF)]

    slots = {}
    sent = {}

    def slot(table, key):
        return table.setdefault(key, len(table))

    def send(key, src, dst, dev, size=1, phase="w", plane=None):
        sent[phase, plane] = sent.get((phase, plane), 0) + size
        pltpu.make_async_remote_copy(
            src_ref=src, dst_ref=dst, send_sem=ssem.at[PHASES[phase]],
            recv_sem=rsem.at[slot(slots, key)], device_id=dev, device_id_type=MESH,
        ).start()

    def recv(key, size=1):
        part = stand_in(size)
        pltpu.make_async_remote_copy(
            src_ref=part, dst_ref=part, send_sem=ssem.at[0],
            recv_sem=rsem.at[slot(slots, key)], device_id=mate, device_id_type=MESH,
        ).wait_recv()

    loads = [
        pltpu.make_async_copy(src, dst, lsem.at[i]) for i, (src, dst) in enumerate((
            (up_ref, uf.at[z, y, c]), (down_ref, vf.at[z, y, c]), (wid_ref, wid_v),
            (tok_ref, rows_v.at[0]), (cot_ref, rows_v.at[1]),
        ))
    ]
    for copy in loads:
        copy.start()

    barrier = pltpu.get_barrier_semaphore()
    for dev in near + xs:
        pl.semaphore_signal(barrier, inc=1, device_id=dev, device_id_type=MESH)

    loads[0].wait()
    loads[1].wait()
    pl.semaphore_wait(barrier, len(near) + len(xs))

    def peer_y(r):
        return ymod(y + r)

    def u_share(k):
        zz = zmod(z + k)
        for r in (1, 3, 2):
            ref = uf.at[zz, y, c]
            send(("uy", k), ref, ref, at(z, peer_y(r), c))

    def u_direct(k):
        ref = uf.at[z, y, c]
        send(("uz", k), ref, ref, at(zmod(z + k), y, c))

    def u_pass(k):
        near, far, cols = (-1, -2, halves(1)) if k > 0 else (1, 2, halves(0))
        ref = uf.at[zmod(z + k), y, c]
        send(("uz", near - k), ref, ref, at(zmod(z + near), y, c))
        ref = uf.at[zmod(z + k), y, c, :, cols]
        send(("uz", 4), ref, ref, at(zmod(z + far), y, c), 0.5)

    def u_recv(k):
        recv(("uz", -k if k != 4 else 4))

    def u_group(k):
        recv(("uy", k), 3)
        zz = zmod(z + k)
        send("wc", uf.at[zz, :, c], uf.at[zz, :, c], mate, 4, "wc")

    def v_mate(r, k):
        ref = vf.at[zmod(z + k), peer_y(r), c]
        send("wc", ref, ref, mate, 1, "wc")

    def v_to(r, k, hop):
        ref = vf.at[zmod(z + k), peer_y(r), c]
        far = k - hop
        send(("vz", r, 4 if abs(far) == 4 else far), ref, ref, at(zmod(z + hop), y, c))

    def v_direct(r):
        for k in (1, -1, 2, -2):
            v_to(r, 0, k)

    def v_recv(r, k):
        recv(("vz", r, k))
        if abs(k) == 2:
            near = -1 if k > 0 else 1
            if (r < 2) == (k < 0):
                v_to(r, k, 2 * near)
            v_to(r, k, near)
        v_mate(r, k)

    own_v = vf.at[z, y, c]
    for r in (1, 3, 2):
        send(("vy", r), own_v, own_v, at(z, peer_y(r), c))
    v_direct(0)
    u_direct(1)
    u_direct(-1)
    u_share(0)
    u_direct(2)
    u_direct(-2)

    for copy in loads[2:]:
        copy.wait()
    wid = wid_v[...]
    level = lax.broadcasted_iota(jnp.int32, (8, ROWS), 0)
    ind = (jnp.broadcast_to(wid, (8, ROWS)) == level).astype(F32)
    ind16 = ind.astype(BF16)
    ia = lax.broadcasted_iota(jnp.int32, (ROWS, ROWS), 0)
    ib = lax.broadcasted_iota(jnp.int32, (ROWS, ROWS), 1)
    above = (ia < ib).astype(F32).astype(BF16)
    below = (ib < ia).astype(F32).astype(BF16)
    eye = (ia == ib).astype(F32).astype(BF16)
    counts = jnp.sum(ind, axis=1, keepdims=True)
    wider = [
        sum([counts[k:k + 1] for k in range(lo, 4)], jnp.zeros((1, 1), F32)) for lo in range(5)
    ]
    pre_row = jnp.dot(ind16, above, preferred_element_type=F32)
    pre_col = lax.dot_general(below, ind16, NT, preferred_element_type=F32)
    ind_col = lax.dot_general(eye, ind16, NT, preferred_element_type=F32)
    rank_row = sum([ind[k:k + 1] * (pre_row[k:k + 1] + wider[k + 1]) for k in range(4)])
    rank_col = sum(
        [ind_col[:, k:k + 1] * (pre_col[:, k:k + 1] + wider[k + 1]) for k in range(4)]
    )
    perm[...] = (ia == rank_row.astype(jnp.int32)).astype(F32).astype(BF16)
    permt[...] = (ib == rank_col.astype(jnp.int32)).astype(F32).astype(BF16)
    mine = pl.ds(pl.multiple_of(hid * COLS, COLS), COLS)
    for a in (0, 1):
        xg[a, :, mine] = jnp.dot(perm[...], rows_v[a], preferred_element_type=F32).astype(BF16)

    def xpart(h, lo, hi):
        return xg.at[:, pl.ds(lo, hi - lo), pl.ds(h * COLS, COLS)]

    def xsend(src, dst, h, lo, hi, key):
        part = xpart(h, lo, hi)
        send(key, part, part, xs[(dst - src) % 4 - 1], (hi - lo) // 32, "x", src)

    @pl.when(hid == 2)
    def _():
        xsend(2, 1, 2, 0, 128, "x0")
        xsend(2, 3, 2, 128, 256, "x0")
        xsend(2, 3, 2, 0, 64, "xm")
        xsend(2, 1, 2, 256, 384, "x1")
        xsend(2, 3, 2, 384, 512, "x1")

    @pl.when(hid == 1)
    def _():
        xsend(1, 0, 1, 0, 256, "x0")
        xsend(1, 2, 1, 0, 64, "xm")
        xsend(1, 3, 1, 0, 64, "xm")
        xsend(1, 0, 1, 256, 512, "x1")

    @pl.when(hid == 3)
    def _():
        xsend(3, 0, 3, 0, 256, "x0")
        xsend(3, 2, 3, 0, 64, "xm")
        xsend(3, 1, 3, 0, 128, "xm")
        xsend(3, 0, 3, 256, 512, "x1")

    @pl.when(hid == 0)
    def _():
        xsend(0, 1, 0, 0, 128, "xm")
        xsend(0, 3, 0, 0, 64, "xm")
        xsend(0, 2, 0, 0, 64, "xm")

    def forward_tokens(part):
        for plane, lo in ((1, 256 * part), (3, 256 * part + 128)):
            @pl.when(hid == plane)
            def _():
                recv(f"x{part}", 4)
                xsend(plane, 0, 2, lo, lo + 128, f"x{part}")

    for r in (3, 1, 2):
        recv(("vy", (4 - r) % 4))
        v_direct(r)
        v_mate(r, 0)
    v_mate(0, 0)
    for k in (1, -1):
        u_recv(k)
        u_share(k)
    for k in (2, -2):
        u_recv(k)
        u_pass(k)
        u_share(k)
    for k in (2, -2, 1, -1):
        v_recv(0, k)
    forward_tokens(0)
    for r in (3, 1, 2):
        for k in (2, -2, 1, -1):
            v_recv(r, k)
    for k in (3, -3, 4):
        u_recv(k)
        u_share(k)
    u_group(0)
    for k in (3, -3, 4):
        v_recv(0, k)
    u_group(1)
    u_group(-1)
    forward_tokens(1)
    u_group(2)
    u_group(-2)
    for r in (3, 1, 2):
        for k in (3, -3, 4):
            v_recv(r, k)
    u_group(3)
    u_group(-3)
    u_group(4)
    recv("wc", 64)

    def units(lo_row, n_row, lo_tile, hi_tile, count):
        rows = pl.ds(lo_row, n_row)

        def body(j, carry):
            cols = pl.ds(pl.multiple_of(j * TILE, TILE), TILE)
            u = uf[:, :, :, :, cols].reshape(D, TILE)
            v = vf[:, :, :, :, cols].reshape(D, TILE)
            pre = jnp.dot(xg[0, rows, :], u, preferred_element_type=F32)
            gh = jnp.dot(xg[1, rows, :], v, preferred_element_type=F32)
            act, slope = gelu_pair(pre)
            pg = gh * slope
            if count is not None:
                row = lax.broadcasted_iota(jnp.int32, (n_row, TILE), 0).astype(F32) + lo_row
                keep = row < count
                act = jnp.where(keep, act, 0.0)
                pg = jnp.where(keep, pg, 0.0)
            hbuf[rows, cols] = act.astype(BF16)
            pbuf[rows, cols] = pg.astype(BF16)
            return carry

        lax.fori_loop(lo_tile, hi_tile, body, 0, unroll=True)

    def outputs(plane, d, lo_row, n_row, n_unit):
        rows = pl.ds(lo_row, n_row)
        for a, val, w in ((0, hbuf, vf), (1, pbuf, uf)):
            wt = w[2 * d:2 * d + 2].reshape(COLS, UNITS)[:, :n_unit]
            out = lax.dot_general(val[rows, :n_unit], wt, NT, preferred_element_type=F32)
            if d == plane:
                ro[plane, a, rows, :] = out.astype(BF16)
            else:
                so[d, a, rows, :] = out.astype(BF16)

    def osend(src, dst, d, lo, hi, via=False):
        rows = pl.ds(lo, hi - lo)
        to = fo.at[:, rows, :] if via else ro.at[src, :, rows, :]
        send(f"f{lo // 256}" if via else "o", so.at[d, :, rows, :], to,
             xs[(dst - src) % 4 - 1], (hi - lo) // 32, "o", src)

    def tile(i):
        return lax.rem(lax.div(z, 2) + (2, 1, 3, 0)[i], 4)

    def grads(plane, n_row, h):
        hc = halves(h)
        for i in range(4):
            dt = tile(i)
            cols = pl.ds(pl.multiple_of(dt * COLS, COLS), COLS)
            zs = pl.ds(2 * dt, 2)
            for a, val in ((1, hbuf), (0, pbuf)):
                g = lax.dot_general(
                    xg[a, :n_row, cols], val[:n_row, hc], TN, preferred_element_type=F32)
                g = g.reshape(2, NY, 2, 16, HALF)
                lane[a, zs, :, :, hc] = jnp.where(c == 0, g[:, :, 0], g[:, :, 1])
                part = pl.ds(32 * a + 8 * dt, 8)
                other = jnp.where(c == 0, g[:, :, 1], g[:, :, 0]).astype(BF16)
                gsend[part, :, hc] = other.reshape(8, 16, HALF)
                send(("gc", h, a, GROUP[i]), gsend.at[part, :, hc], grecv.at[part, :, hc], mate,
                     4, "g", plane)

    def mate_grads(h, a, group):
        recv(("gc", h, a, group), 8 if group == 1 else 4)

    others = (
        (1, 128, 8, (0, 3, 2, 1)), (2, 64, 6, (0, 1, 3, 2)), (3, 64, 6, (1, 0, 2, 3)),
    )

    def row_outputs(lo, n_unit, dests=(2, 1, 3, 0)):
        for d in dests:
            outputs(0, d, lo, 256, n_unit)
            if d == 2:
                osend(0, 1, 2, lo, lo + 128, True)
                osend(0, 3, 2, lo + 128, lo + 256, True)
            elif d:
                osend(0, d, d, lo, lo + 256)

    @pl.when(hid == 0)
    def _():
        recv("x0", 24)
        units(0, 256, 2, 4, wider[1])
        grads(0, 256, 1)
        units(0, 256, 0, 2, None)
        row_outputs(0, UNITS, (2,))

    for plane, n_row, n_in, dests in others:
        @pl.when(hid == plane)
        def _():
            recv("xm", n_in)
            count = wider[min(plane + 1, 3)]
            units(0, n_row, 2, 4, count)
            grads(plane, n_row, 1)
            units(0, n_row, 0, 2, count)
            for d in dests:
                outputs(plane, d, 0, n_row, UNITS)
                if d != plane:
                    osend(plane, d, d, 0, n_row)

    def rest_of_rows():
        @pl.when(hid == 0)
        def _():
            recv("x1", 24)
            units(256, 256, 0, 2, None)
            grads(0, 512, 0)
            row_outputs(0, UNITS, (1, 3, 0))

        for plane, n_row, _, _ in others:
            @pl.when(hid == plane)
            def _():
                grads(plane, n_row, 0)

    def forward_outputs(part):
        for plane, lo in ((1, 256 * part), (3, 256 * part + 128)):
            @pl.when(hid == plane)
            def _():
                recv(f"f{part}", 4)
                rows = pl.ds(lo, 128)
                send("o", fo.at[:, rows, :], ro.at[0, :, rows, :], xs[(2 - plane) % 4 - 1], 4,
                     "o", plane)

    def total(h, a, zz, yy):
        hc = halves(h)
        return lane[a, zz, yy, :, hc] + grecv[32 * a + 4 * zz + yy, :, hc].astype(F32)

    def steps(p, d):
        return 4 if p == d else 3

    def ring(h, s):
        hc = halves(h)
        for p in (0, 1):
            for d in (0, 1):
                first = 4 - steps(p, d)
                ys = pl.ds(2 * p, 2)
                if s > first:
                    recv(("v", h, p, d, s - 1))
                if s < first:
                    continue
                zz = zmod(z + 4 - s) if d == 0 else zmod(z - 4 + s)
                for r in (2 * p, 2 * p + 1):
                    val = total(h, 1, zz, peer_y(r))
                    if s > first:
                        val = val + rv[d, s - 1, r, :, hc].astype(F32)
                    sv[d, s, r, :, hc] = val.astype(BF16)
                send(("v", h, p, d, s), sv.at[d, s, ys, :, hc], rv.at[d, s, ys, :, hc],
                     zp if d == 0 else zm, 1, "r")

    def ring_end(h):
        hc = halves(h)
        for p in (1, 0):
            for d in (0, 1):
                recv(("v", h, p, d, 3))
            for r in (2 * p + 1, 2 * p):
                val = total(h, 1, z, peer_y(r))
                for d in (0, 1):
                    val = val + rv[d, 3, r, :, hc].astype(F32)
                if r:
                    svy[r, :, hc] = val.astype(BF16)
                    send(("vw", h), svy.at[r, :, hc], rvy.at[r, :, hc], at(z, peer_y(r), c),
                         0.5, "r")
                else:
                    vz[:, hc] = val

    def up_share(h, k):
        hc = halves(h)
        for r in (1, 3, 2):
            su1[k + 3, r, :, hc] = total(h, 0, zmod(z + k), peer_y(r)).astype(BF16)
            send(("uu", h, k), su1.at[k + 3, r, :, hc], ru1.at[k + 3, r, :, hc],
                 at(z, peer_y(r), c), 0.5, "r")

    def up_sum(h, k):
        hc = halves(h)
        val = total(h, 0, zmod(z + k), y)
        recv(("uu", h, k), 1.5)
        for r in (1, 3, 2):
            val = val + ru1[k + 3, r, :, hc].astype(F32)
        return val

    def up_send(h, k, val, key, hop):
        hc = halves(h)
        suz[k + 3, :, hc] = val.astype(BF16)
        send(key, suz.at[k + 3, :, hc], ruz.at[k + 3, :, hc], at(zmod(z + hop), y, c), 0.5, "r")

    def up_far(h):
        up_send(h, 4, up_sum(h, 4), ("uf", h, 4), 2 if h == 0 else -2)
        up_send(h, 3, up_sum(h, 3), ("uf", h, 3), 1)
        up_send(h, -3, up_sum(h, -3), ("uf", h, -3), -1)

    def up_near(h):
        for k in (1, -1):
            up_send(h, k, up_sum(h, k), ("ue", h), k)

    def up_two(h):
        hc = halves(h)
        for k, far in ((2, 3), (-2, -3)):
            val = up_sum(h, k)
            recv(("uf", h, far), 0.5)
            val = val + ruz[far + 3, :, hc].astype(F32)
            if (k == 2) == (h == 0):
                recv(("uf", h, 4), 0.5)
                val = val + ruz[7, :, hc].astype(F32)
            up_send(h, k, val, ("ue", h), k)

    def start_half(h):
        mate_grads(h, 1, 0)
        ring(h, 0)
        mate_grads(h, 0, 0)
        up_share(h, 4)
        mate_grads(h, 0, 1)
        for k in (3, -3, 2, -2):
            up_share(h, k)
        mate_grads(h, 0, 2)
        for k in (1, -1, 0):
            up_share(h, k)
        mate_grads(h, 1, 1)
        mate_grads(h, 1, 2)

    start_half(1)
    rest_of_rows()
    start_half(0)
    ring(1, 1)
    up_far(1)

    @pl.when(hid == 0)
    def _():
        row_outputs(256, HALF)

    ring(0, 1)
    ring(1, 2)
    up_near(1)
    up_far(0)
    forward_outputs(0)
    ring(0, 2)
    ring(1, 3)
    up_two(1)
    up_near(0)
    ring(0, 3)
    ring_end(1)
    uy[:, halves(1)] = up_sum(1, 0)
    up_two(0)
    forward_outputs(1)
    uy[:, halves(0)] = up_sum(0, 0)
    ring_end(0)

    for plane, n_in in ((0, 8), (1, 20), (2, 22), (3, 22)):
        @pl.when(hid == plane)
        def _():
            recv("o", n_in)

    for a, ref in ((0, mixed_ref), (1, gtok_ref)):
        top = ro[0, a, 0:128].astype(F32) + ro[1, a, 0:128].astype(F32)
        wide = top[:64] + ro[2, a, 0:64].astype(F32) + ro[3, a, 0:64].astype(F32)
        ro[0, a, 0:128] = jnp.concatenate([wide, top[64:]], axis=0).astype(BF16)
        ref[...] = jnp.dot(permt[...], ro[0, a], preferred_element_type=F32).astype(BF16)

    for h in (1, 0):
        hc = halves(h)
        recv(("vw", h), 1.5)
        val = vz[:, hc]
        for r in (1, 3, 2):
            val = val + rvy[r, :, hc].astype(F32)
        gdown_ref[:, hc] = val
        recv(("ue", h), 2)
        val = uy[:, hc]
        for k in (1, -1, 2, -2):
            val = val + ruz[k + 3, :, hc].astype(F32)
        gup_ref[:, hc] = val

    def left(phase, plane):
        part = stand_in(sent[phase, plane])
        pltpu.make_async_remote_copy(
            src_ref=part, dst_ref=part, send_sem=ssem.at[PHASES[phase]], recv_sem=rsem.at[0],
            device_id=mate, device_id_type=MESH,
        ).wait_send()

    for phase in ("w", "wc", "r"):
        left(phase, None)
    for plane in range(4):
        @pl.when(hid == plane)
        def _():
            for phase in ("x", "o", "g"):
                left(phase, plane)
    assert len(slots) == N_SEM, len(slots)


def store(*refs):
    sem = refs[-1]
    copies = [pltpu.make_async_copy(refs[i], refs[4 + i], sem.at[i]) for i in range(4)]
    for copy in copies:
        copy.start()
    for copy in copies:
        copy.wait()


def per_device(tokens, width_index, up_weight, down_weight, cotangent):
    vm = pl.BlockSpec(memory_space=pltpu.VMEM)
    hbm = pl.BlockSpec(memory_space=pltpu.HBM)
    block = (16, UNITS)
    shapes = [((ROWS, COLS), BF16), ((ROWS, COLS), BF16), (block, F32), (block, F32)]

    def buf(*shape):
        return pltpu.VMEM(shape, BF16)

    results = pl.pallas_call(
        kernel,
        out_shape=tuple(pltpu.VMEM(*shape) for shape in shapes),
        in_specs=[hbm] * 5,
        out_specs=(vm,) * 4,
        scratch_shapes=[
            buf(NZ, NY, 2, *block), buf(NZ, NY, 2, *block),
            buf(2, ROWS, D), buf(ROWS, UNITS), buf(ROWS, UNITS),
            buf(4, 2, ROWS, COLS), buf(4, 2, ROWS, COLS), buf(2, ROWS, COLS),
            buf(ROWS, ROWS), buf(ROWS, ROWS),
            buf(64, *block), buf(64, *block),
            pltpu.VMEM((2, NZ, NY, *block), F32),
            buf(2, ROWS, COLS), pltpu.VMEM((1, ROWS), jnp.int32),
            buf(2, 4, NY, *block), buf(2, 4, NY, *block),
            buf(NZ, NY, *block), buf(NZ, NY, *block),
            buf(NZ, *block), buf(NZ, *block),
            buf(NY, *block), buf(NY, *block),
            pltpu.VMEM(block, F32), pltpu.VMEM(block, F32),
            pltpu.SemaphoreType.DMA((len(PHASES),)), pltpu.SemaphoreType.DMA((N_SEM,)),
            pltpu.SemaphoreType.DMA((5,)),
        ],
        compiler_params=pltpu.CompilerParams(
            collective_id=0, has_side_effects=True, vmem_limit_bytes=48 * 1024 * 1024,
        ),
    )(*[
        pltpu.with_memory_space_constraint(x, pltpu.HBM)
        for x in (tokens, width_index.reshape(1, ROWS), up_weight, down_weight.T, cotangent)
    ])
    mixed, gtok, gup, gdown = pl.pallas_call(
        store,
        out_shape=tuple(jax.ShapeDtypeStruct(*shape) for shape in shapes),
        in_specs=[vm] * 4,
        out_specs=(hbm,) * 4,
        scratch_shapes=[pltpu.SemaphoreType.DMA((4,))],
    )(*[pltpu.with_memory_space_constraint(x, pltpu.VMEM) for x in results])
    return mixed, gtok, gup, gdown.T


def solution(mesh):
    placed = (P("tok", "hid"), P("tok"), P("tok", "hid"), P("hid", "tok"), P("tok", "hid"))
    return jax.shard_map(
        per_device,
        mesh=mesh,
        in_specs=placed,
        out_specs=(P("tok", "hid"), P("tok", "hid"), P("tok", "hid"), P("hid", "tok")),
        check_vma=False,
    )
```
